256 devices in a mesh: store: 32 (over z, x), head: 8 (over y, core).
Axes of the slice: x: 4, y: 4, z: 8, core: 2. Of those that a mesh axis runs over, the one named last changes fastest.
Arguments:
- hidden: bfloat16 [32, 128, 8192], P('store'), may hold values from -6 to 6
- w_query: bfloat16 [8192, 4096], P('store', 'head'), may hold values from -0.0625 to 0.0625
- w_key_value: bfloat16 [8192, 2048], P('store', 'head'), may hold values from -0.0625 to 0.0625
- block_kv: bfloat16 [64, 512, 2048], P('store', None, 'head'), may hold values from -68 to 68
- history_kv: bfloat16 [32, 512, 2048], P('store', 'head'), may hold values from -6 to 6
- block_lists: int32 [32, 8], replicated, may hold values from 0 to 63, as said below
- sel_pos: int32 [32, 128], P('store'), may hold values from 0 to 4095, as said below
- hist_len: int32 [32], P('store'), may hold values from 1 to 512, 8192 in all
Outputs:
- attended: bfloat16 [32, 128, 4096], P('store', None, 'head')
The draws below stay inside these ranges and needn't reach their ends.
Inputs may be any that keep to these rules, and one draw needn't show every extreme that they name: `block_lists`: of the 8 blocks named by the requests of one index of store (requests r with r // 1 equal), at most 1 have the same owner block // 2, and some owner is named exactly 1 times. `sel_pos`: the positions of one request are distinct and include 8 * 512 - 1.
All inputs are finite; a program needn't handle non-finite values. No bound on the sum of `hist_len` on one device may be relied on, other than what follows from the above.
Results may differ from the reference program's by a relative error of at most 0.011.
The reference program's roundings to bfloat16 on the way count: a program that leaves them out, or rounds other values in their place, can miss the bound.
Values may be sent and summed in bfloat16 or wider, within the bound.
No kernel may reach another device: no remote copies, remote signals or barrier semaphores. Data moves between devices by JAX's collectives and lax.ppermute only.
A program may use at most 128 MiB of HBM per device.

```python
import math
import jax
import jax.numpy as jnp
import numpy as np
from jax import lax

D = 8192
HEAD_DIM = 128
QPER = 4
BLOCK = 512
RET = 8
CH_DEV = 2
REQ_DEV = 1
SEL = 128
HIST = 512
KVH = 8
REQS = 32
NCHUNK = 64
N_STORE = 32


def draw_block_lists(key, part):
    key = jax.random.fold_in(key, 11)
    per_group = REQ_DEV * RET

    def one_group(group_id):
        group_key = jax.random.fold_in(key, group_id)
        shuffled = jax.random.permutation(jax.random.fold_in(group_key, 1), N_STORE)
        owners = shuffled[jnp.arange(per_group) % N_STORE]
        local_ids = jax.random.randint(jax.random.fold_in(group_key, 2), (per_group,), 0, CH_DEV)
        return (owners * CH_DEV + local_ids).astype(jnp.int32)
    table = jax.vmap(one_group)(jnp.arange(N_STORE))
    return table.reshape(REQS, RET).astype(jnp.int32)


def draw_sel_pos(key, part):
    key = jax.random.fold_in(key, 12)
    context = RET * BLOCK

    def one_request(request_id):
        request_key = jax.random.fold_in(key, request_id)
        shuffled = jax.random.permutation(request_key, context - 1)[:SEL - 1]
        return jnp.concatenate([jnp.full((1,), context - 1, jnp.int32), shuffled.astype(jnp.int32)])
    return jax.vmap(one_request)(jnp.arange(REQS)).astype(jnp.int32)


def draw_block_kv(key, part):
    key = jax.random.fold_in(key, 13)
    shape = (NCHUNK, BLOCK, KVH * 2 * HEAD_DIM)
    values = jnp.clip(jax.random.normal(key, shape, jnp.float32), -4.0, 4.0)
    return values.astype(jnp.bfloat16)


def block_levels(key, dims, split, least, top_value):
    gain, own = 1.0, jax.random.fold_in(key, 6)
    for axis_at, shards_of in split:
        draws = jnp.exp(jax.random.uniform(jax.random.fold_in(own, axis_at), (shards_of,), jnp.float32, least / len(split), top_value / len(split)))
        gain = gain * jnp.repeat(draws, dims[axis_at] // shards_of).reshape([-1 if axis == axis_at else 1 for axis in range(len(dims))])
    return gain


def profile(count, total, reach, slope):
    weights = [(1 << 20) // math.isqrt(grade ** slope) + 1 for grade in range(2, count + 1)]
    surplus, counts = total - reach - (count - 1), [1] * (count - 1)
    while surplus > 0:
        candidates = [i for i in range(count - 1) if counts[i] < reach]
        pool, left = sum([weights[i] for i in candidates]), surplus
        for i in candidates:
            extra = min(reach - counts[i], max(1, left * weights[i] // pool), surplus)
            counts[i] = counts[i] + extra
            surplus = surplus - extra
    return np.array([reach] + counts)


def uneven_parts(stream_key, number_of, total, reach, slope):
    if number_of == 2:
        one = jax.random.randint(stream_key, (), max(1, total - reach), min(reach, total - 1) + 1)
        return jnp.stack([one, total - one])
    tallies = jnp.asarray(profile(number_of, total, reach, slope), jnp.int32)
    pairs = (number_of - 1) // 2
    donor, receiver = tallies[1:1 + 2 * pairs:2], tallies[2:2 + 2 * pairs:2]
    margin = jnp.minimum(donor - 1, reach - receiver)
    shifted = jax.random.randint(jax.random.fold_in(stream_key, 1), (pairs,), 0, 1 << 20) % (margin + 1)
    tallies = tallies.at[1:1 + 2 * pairs:2].set(donor - shifted).at[2:2 + 2 * pairs:2].set(receiver + shifted)
    return tallies[jax.random.permutation(jax.random.fold_in(stream_key, 2), number_of)]


def normal_values(stream_key, extent, scale, reach, cuts=(), kind=jnp.bfloat16):
    loudness = block_levels(stream_key, extent, cuts, -0.22, 0.18) if cuts else 1.0
    result = jax.random.normal(stream_key, extent, jnp.float32) * scale * loudness
    return jnp.minimum(jnp.maximum(result, -reach), reach).astype(kind)


def setup_inputs(seed: int = 0) -> dict:
    arg_keys = jax.random.split(jax.random.key(seed), 9)
    return {
        "hidden": normal_values(arg_keys[0], (REQS, SEL, D), 1.0, 6.0, ((0, 32),)),
        "w_query": normal_values(arg_keys[1], (D, KVH * QPER * HEAD_DIM), D ** -0.5, 0.0625, ((0, 32), (1, 8))),
        "w_key_value": normal_values(arg_keys[2], (D, KVH * 2 * HEAD_DIM), D ** -0.5, 0.0625, ((0, 32), (1, 8))),
        "block_kv": draw_block_kv(jax.random.fold_in(arg_keys[8], 71), 0),
        "history_kv": normal_values(arg_keys[4], (REQS, HIST, KVH * 2 * HEAD_DIM), 1.0, 6.0, ((0, 32), (1, 8))),
        "block_lists": draw_block_lists(jax.random.fold_in(arg_keys[8], 71), 0),
        "sel_pos": draw_sel_pos(jax.random.fold_in(arg_keys[8], 71), 0),
        "hist_len": uneven_parts(arg_keys[7], REQS, REQS * HIST // 2, HIST, 1).astype(jnp.int32),
    }


def rotate(values, position):
    halfway = values.shape[-1] // 2
    inverse = 500000.0 ** (-(jnp.arange(halfway, dtype=jnp.float32) * 2.0 / values.shape[-1]))
    angles = position.astype(jnp.float32)[:, None] * inverse
    shape_out = (angles.shape[0],) + (1,) * (values.ndim - 2) + (halfway,)
    cosine = jnp.cos(angles).reshape(shape_out)
    sine_part = jnp.sin(angles).reshape(shape_out)
    leading = values[..., :halfway]
    trailing = values[..., halfway:]
    return jnp.concatenate([leading * cosine - trailing * sine_part, trailing * cosine + leading * sine_part], -1)


def reference(hidden, w_query, w_key_value, block_kv, history_kv, block_lists, sel_pos, hist_len):
    score_scale = HEAD_DIM ** -0.5
    context = RET * BLOCK

    def one_request(inputs):
        states, chosen, positions, length, history = inputs
        qraw = jnp.dot(states, w_query, preferred_element_type=jnp.float32)
        fresh = jnp.dot(states, w_key_value, preferred_element_type=jnp.float32).astype(jnp.bfloat16)
        query_pos = length + positions
        queries = rotate(qraw.reshape(SEL, KVH, QPER, HEAD_DIM), query_pos).astype(jnp.bfloat16)
        cached = jnp.take(block_kv, chosen, axis=0).reshape(context, KVH * 2 * HEAD_DIM)
        blended = cached.at[positions].set(fresh).reshape(context, KVH, 2, HEAD_DIM)
        block_pos = length + jnp.arange(context, dtype=jnp.int32)
        ctx_keys = rotate(blended[:, :, 0].astype(jnp.float32), block_pos).astype(jnp.bfloat16)
        past = history.reshape(HIST, KVH, 2, HEAD_DIM)
        keys = jnp.concatenate([past[:, :, 0], ctx_keys], 0)
        values = jnp.concatenate([past[:, :, 1], blended[:, :, 1]], 0)
        slots = jnp.arange(HIST, dtype=jnp.int32)
        key_pos = jnp.concatenate([slots, block_pos], 0)
        live = jnp.concatenate([slots < length, block_pos >= 0], 0)
        allowed = live[None, :] & (key_pos[None, :] <= query_pos[:, None])
        scores = jnp.einsum('shqd,khd->hqsk', queries.astype(jnp.float32), keys.astype(jnp.float32)) * score_scale
        scores = jnp.where(allowed[None, None], scores, -jnp.inf)
        row_max = jnp.max(scores, axis=-1, keepdims=True)
        weights = jnp.exp(scores - row_max)
        weights = (weights / jnp.sum(weights, axis=-1, keepdims=True)).astype(jnp.bfloat16)
        mixed = jnp.einsum('hqsk,khd->shqd', weights.astype(jnp.float32), values.astype(jnp.float32))
        return mixed.astype(jnp.bfloat16).reshape(SEL, KVH * QPER * HEAD_DIM)

    return lax.map(one_request, (hidden, block_lists, sel_pos, hist_len, history_kv))
```

```python
import jax
import jax.numpy as jnp
import numpy as np
from jax import lax
from jax.sharding import Mesh
from jax.sharding import PartitionSpec as P

NZ, NX, NH = 8, 4, 8
SEL, HEAD, QPER, BLOCK, RET, HIST = 128, 128, 4, 512, 8, 512
CONTEXT = RET * BLOCK
PIECE = BLOCK // NX
FAR = 1 << 20
INVERSE = (500000.0 ** (-(np.arange(64, dtype=np.float64) * 2.0 / 128))).astype(np.float32)


def angles(position):
    return position.astype(jnp.float32)[:, None] * jnp.asarray(INVERSE)


def rotate(values, cosine, sine):
    a, b = values[..., :64], values[..., 64:]
    return jnp.concatenate([a * cosine - b * sine, b * cosine + a * sine], -1)


def per_device(hidden, w_query, w_key_value, block_kv, history_kv, block_lists, sel_pos, hist_len):
    z, x = lax.axis_index("z"), lax.axis_index("x")
    length, sel = hist_len[0], sel_pos[0]

    pieces = block_kv.reshape(2, NX, PIECE, 2 * HEAD).transpose(1, 0, 2, 3)
    pieces = lax.all_to_all(pieces, "x", 0, 0, tiled=True)
    weights = lax.all_gather(jnp.concatenate([w_query, w_key_value], 1), "z", axis=0, tiled=True)
    pieces = lax.all_gather(pieces, "z", axis=0, tiled=True)
    pieces = pieces.reshape(2 * NZ * NX, PIECE, 2 * HEAD)
    row_lists = lax.dynamic_slice_in_dim(block_lists, z * NX, NX, 0).reshape(-1)

    rows = hidden[0].reshape(SEL, NZ, NX, 256).transpose(2, 0, 1, 3).reshape(NX, SEL, NZ * 256)
    rows = lax.all_to_all(rows, "x", 0, 0, tiled=True)
    partial = jnp.dot(rows.reshape(NX * SEL, NZ * 256), weights, preferred_element_type=jnp.float32)
    partial = lax.all_to_all(partial.reshape(NX, SEL, -1), "x", 0, 0, tiled=True)
    projected = jnp.sum(partial, 0)
    qraw, fresh = projected[:, : QPER * HEAD], projected[:, QPER * HEAD :].astype(jnp.bfloat16)

    past = history_kv[0].reshape(HIST // NH, NH, 2 * HEAD).transpose(1, 0, 2)
    past = lax.all_to_all(past, "head", 0, 0, tiled=True).reshape(HIST, 2 * HEAD)

    cached = pieces[row_lists].reshape(NX, RET, PIECE, 2 * HEAD)
    cached = lax.all_to_all(cached, "x", 0, 0, tiled=True).reshape(CONTEXT, 2 * HEAD)
    order = np.arange(CONTEXT, dtype=np.int32).reshape(RET, NX, PIECE).transpose(1, 0, 2).reshape(-1)
    place = jnp.asarray(order)

    replaced = jnp.any(place[:, None] == sel[None, :], axis=1)
    slots = jnp.arange(HIST, dtype=jnp.int32)
    key_pos = jnp.concatenate(
        [jnp.where(slots < length, -1, FAR), jnp.where(replaced, FAR, place), sel]
    )
    qangle, cangle = angles(length + sel), angles(length + place)
    qcos, qsin, ccos, csin = jnp.cos(qangle), jnp.sin(qangle), jnp.cos(cangle), jnp.sin(cangle)

    queries = rotate(qraw.reshape(SEL, QPER, HEAD), qcos[:, None], qsin[:, None])
    queries = queries.astype(jnp.bfloat16).transpose(1, 0, 2)
    fresh_keys = rotate(fresh[:, :HEAD].astype(jnp.float32), qcos, qsin).astype(jnp.bfloat16)
    ctx_keys = rotate(cached[:, :HEAD].astype(jnp.float32), ccos, csin).astype(jnp.bfloat16)
    keys = jnp.concatenate([past[:, :HEAD], ctx_keys, fresh_keys], 0)
    values = jnp.concatenate([past[:, HEAD:], cached[:, HEAD:], fresh[:, HEAD:]], 0)
    scores = jnp.einsum("qsd,kd->qsk", queries, keys, preferred_element_type=jnp.float32)
    scores = scores * (HEAD ** (-0.5))
    scores = jnp.where((key_pos[None, :] <= sel[:, None])[None], scores, -jnp.inf)
    top = jnp.max(scores, axis=-1, keepdims=True)
    mass = jnp.exp(scores - top)
    mass = (mass / jnp.sum(mass, axis=-1, keepdims=True)).astype(jnp.bfloat16)
    mixed = jnp.einsum("qsk,kd->sqd", mass, values, preferred_element_type=jnp.float32)
    return mixed.astype(jnp.bfloat16).reshape(1, SEL, QPER * HEAD)


def solution(mesh):
    split = Mesh(mesh.devices.reshape(NZ, NX, NH), ("z", "x", "head"))
    store = ("z", "x")
    in_specs = (
        P(store, None, None),
        P(store, "head"),
        P(store, "head"),
        P(store, None, "head"),
        P(store, "head", None),
        P(),
        P(store, None),
        P(store),
    )
    return jax.shard_map(
        per_device, mesh=split, in_specs=in_specs, out_specs=P(store, None, "head"), check_vma=False
    )
```

```python
import functools

import jax
import jax.numpy as jnp
import numpy as np
from jax import lax
from jax.experimental import pallas as pl
from jax.experimental.pallas import tpu as pltpu
from jax.sharding import Mesh
from jax.sharding import PartitionSpec as P

NZ, NX, NH = 8, 4, 8
SEL, HEAD, QPER, BLOCK, RET, HIST = 128, 128, 4, 512, 8, 512
CONTEXT = RET * BLOCK
PIECE = BLOCK // NX
WIDE = (QPER + 2) * HEAD
FAR = 1 << 20
FREE = pl.CostEstimate(flops=0, bytes_accessed=0, transcendentals=0)
COST = pl.CostEstimate(flops=5 * 10**10, bytes_accessed=1 << 20, transcendentals=0)
HALF = SEL // 2
KEYS = HIST + CONTEXT + SEL
INVERSE = (500000.0 ** (-(np.arange(64, dtype=np.float64) * 2.0 / 128))).astype(np.float32)
INVERSE = np.concatenate([INVERSE, INVERSE])
UP = [(i, (i + 1) % NZ) for i in range(NZ)]
DOWN = [(i, (i - 1) % NZ) for i in range(NZ)]
SMEM = pl.BlockSpec(memory_space=pltpu.SMEM)
VMEM = pl.BlockSpec(memory_space=pltpu.VMEM)
ANY = pl.BlockSpec(memory_space=pltpu.HBM)
PARAMS = pltpu.CompilerParams(vmem_limit_bytes=56 << 20)


def kernel_call(body, out, inputs, smem=0, scratch=()):
    many = isinstance(out, (list, tuple))
    return pl.pallas_call(
        body,
        out_shape=out,
        in_specs=[SMEM] * smem + [VMEM] * (len(inputs) - smem),
        out_specs=[VMEM] * len(out) if many else VMEM,
        scratch_shapes=scratch,
        compiler_params=PARAMS,
        cost_estimate=FREE,
    )(*inputs)


def after(value, *others):
    return lax.optimization_barrier((value, *others))[0]


def turn(values, cosine, sine):
    return values * cosine + pltpu.roll(values, 64, 1) * sine


def prepare_kernel(
    z_ref, head_ref, hidden, w_query, w_key_value, block, history,
    both, pieces, rows, past, held_both, held_pieces, held_rows, held_past, sems,
):
    loads = [
        [
            (w_query, held_both.at[:, : QPER * HEAD]),
            (w_key_value, held_both.at[:, QPER * HEAD :]),
        ],
        [],
        [],
        [(history.at[:, i * 256 : (i + 1) * 256], held_past.at[i]) for i in range(NH)],
    ]
    for x in range(NX):
        for kind in range(2):
            part = block.at[:, x * PIECE : (x + 1) * PIECE, kind * HEAD : (kind + 1) * HEAD]
            loads[1].append((part, held_pieces.at[x, kind]))
    mine = pl.ds(pl.multiple_of((head_ref[0] & 1) * HALF, HALF), HALF)
    for hop in range(NZ):
        chunk = ((z_ref[0] + hop) & (NZ - 1)) * NX
        for x in range(NX):
            at = pl.multiple_of((chunk + x) * 256, 256)
            to = held_rows.at[x, :, hop * 256 : (hop + 1) * 256]
            loads[2].append((hidden.at[mine, pl.ds(at, 256)], to))
    loads = [
        [pltpu.make_async_copy(*pair, sems.at[group]) for pair in pairs]
        for group, pairs in enumerate(loads)
    ]
    for group in loads:
        for load in group:
            load.start()
    stores = []
    pairs = (held_both, both), (held_pieces, pieces), (held_rows, rows), (held_past, past)
    for group, pair in enumerate(pairs):
        for load in loads[group]:
            load.wait()
        stores.append(pltpu.make_async_copy(*pair, sems.at[4 + group]))
        stores[-1].start()
    for store in stores:
        store.wait()


def waves(position, inverse):
    angle = position.astype(jnp.float32) * inverse
    turns = jnp.floor(angle * np.float32(2 / np.pi) + 0.5)
    rest = angle - turns * np.float32(1.5703125)
    rest = rest - turns * np.float32(4.837512969970703125e-4)
    rest = rest - turns * np.float32(7.54978995489188216e-8)
    square = rest * rest
    sine = np.float32(-1.9515295891e-4) * square + np.float32(8.3321608736e-3)
    sine = (sine * square + np.float32(-1.6666654611e-1)) * square * rest + rest
    cosine = np.float32(2.443315711809948e-5) * square + np.float32(-1.388731625493765e-3)
    cosine = (cosine * square + np.float32(4.166664568298827e-2)) * square * square
    cosine = cosine - np.float32(0.5) * square + np.float32(1.0)
    first = lax.broadcasted_iota(jnp.int32, angle.shape, 1) < 64
    quarter = turns.astype(jnp.int32) + jnp.where(first, 1, 0)
    wave = jnp.where((quarter & 1) == 1, cosine, sine)
    wave = jnp.where((quarter & 2) == 2, -wave, wave)
    other = pltpu.roll(wave, 64, 1)
    return jnp.where(first, wave, other), jnp.where(first, -other, wave)


def pick_kernel(kind, z_ref, lists_ref, *refs):
    sources, out, held, sems = refs[:NZ], *refs[NZ:]
    z = z_ref[0]

    def part(x):
        return pl.ds(x * RET, RET)

    def leaf(at, away, inner, low, high):
        if high - low == 1:
            to = held.at[at]
            pltpu.make_async_copy(sources[low].at[inner], to, sems.at[at >> 3]).start()
            return
        middle = (low + high) // 2

        @pl.when(away < middle)
        def _():
            leaf(at, away, inner, low, middle)

        @pl.when(away >= middle)
        def _():
            leaf(at, away, inner, middle, high)

    def one(at, _):
        block = lists_ref[z * NX + (at >> 3), at & 7]
        inner = ((block & 6) << 1) + 2 * kind + (block & 1)
        leaf(at, ((block >> 3) - z) & (NZ - 1), inner, 0, NZ)
        return 0

    lax.fori_loop(0, NX * RET, one, 0, unroll=4)
    stores = []
    for x in range(NX):
        pltpu.make_async_copy(held.at[part(x)], held.at[part(x)], sems.at[x]).wait()
        stores.append(pltpu.make_async_copy(held.at[part(x)], out.at[part(x)], sems.at[NX + x]))
        stores[-1].start()
    for store in stores:
        store.wait()


def pick(z, block_lists, sources, kind):
    out = pl.pallas_call(
        functools.partial(pick_kernel, kind),
        out_shape=jax.ShapeDtypeStruct((NX * RET, PIECE, HEAD), jnp.bfloat16),
        in_specs=[SMEM, SMEM] + [ANY] * NZ,
        out_specs=ANY,
        scratch_shapes=[
            pltpu.VMEM((NX * RET, PIECE, HEAD), jnp.bfloat16),
            pltpu.SemaphoreType.DMA((2 * NX,)),
        ],
        compiler_params=PARAMS,
        cost_estimate=FREE,
    )(z, block_lists, *sources)
    return out.reshape(NX, RET, PIECE, HEAD)


def project_kernel(head_ref, received, swapped, *refs):
    weights, out, whole, rows, total, sems = refs[:NZ], *refs[NZ:]
    core = head_ref[0] & 1
    loads = [
        pltpu.make_async_copy(weights[hop], whole.at[pl.ds(hop * 256, 256)], sems.at[0])
        for hop in range(NZ)
    ]
    for x in range(NX):
        for source, half in ((received, core), (swapped, 1 - core)):
            at = pl.ds(pl.multiple_of(x * SEL + half * HALF, HALF), HALF)
            loads.append(pltpu.make_async_copy(source.at[x], rows.at[at], sems.at[0]))
    for load in loads:
        load.start()
    for load in loads:
        load.wait()
    stores = []
    for at in range(0, WIDE, 256):
        part = jnp.dot(rows[...], whole[:, at : at + 256], preferred_element_type=jnp.float32)
        total[:, :, at : at + 256] = part.reshape(NX, SEL, 256)
        columns = pl.ds(at, 256)
        stores.append(
            pltpu.make_async_copy(total.at[:, :, columns], out.at[:, :, columns], sems.at[1])
        )
        stores[-1].start()
    for store in stores:
        store.wait()


def queries_kernel(length_ref, partial_ref, column_ref, inverse_ref, query_ref, key_ref, value_ref):
    cosine, sine = waves(column_ref[...] + length_ref[0], inverse_ref[...])
    for part in range(QPER + 2):
        at = slice(part * HEAD, (part + 1) * HEAD)
        total = partial_ref[0, :, at] + partial_ref[1, :, at]
        total = total + partial_ref[2, :, at] + partial_ref[3, :, at]
        if part < QPER:
            query_ref[part * SEL : (part + 1) * SEL] = turn(total, cosine, sine).astype(jnp.bfloat16)
        elif part == QPER:
            fresh = total.astype(jnp.bfloat16).astype(jnp.float32)
            key_ref[...] = turn(fresh, cosine, sine).astype(jnp.bfloat16)
        else:
            value_ref[...] = total.astype(jnp.bfloat16)


def weigh_kernel(
    length_ref, query_ref, raw_ref, past_ref, fresh_ref, row_ref, column_ref, inverse_ref,
    out, raw, keys, place, scores, mass, sem, out_sem,
):
    fetch = pltpu.make_async_copy(raw_ref, raw, sem)
    fetch.start()
    length, inverse, column = length_ref[0], inverse_ref[...], column_ref[...]
    slots = lax.broadcasted_iota(jnp.int32, (1, HIST), 1)
    place[:, :HIST] = jnp.where(slots < length, -1, FAR)
    place[:, HIST + CONTEXT :] = row_ref[...]
    keys[:HIST] = past_ref[:, :HEAD]
    keys[HIST + CONTEXT :] = fresh_ref[...]
    fetch.wait()

    def rotate(step, _):
        rows = lax.broadcasted_iota(jnp.int32, (4 * PIECE, 1), 0)
        base = (step & 1) * (4 * BLOCK) + (step >> 1) * PIECE
        rows = base + (rows >> 7) * BLOCK + (rows & 127)
        at = pl.multiple_of(step * (4 * PIECE), 4 * PIECE)
        cosine, sine = waves(rows + length, inverse)
        key = turn(raw[pl.ds(at, 4 * PIECE)].astype(jnp.float32), cosine, sine)
        keys[pl.ds(at + HIST, 4 * PIECE)] = key.astype(jnp.bfloat16)
        here = lax.broadcasted_iota(jnp.int32, (1, 4 * PIECE), 1)
        here = base + (here >> 7) * BLOCK + (here & 127)
        hits = jnp.max(jnp.where(column == here, 1, 0), axis=0, keepdims=True)
        place[:, pl.ds(at + HIST, 4 * PIECE)] = jnp.where(hits > 0, FAR, here)
        return 0

    lax.fori_loop(0, CONTEXT // (4 * PIECE), rotate, 0)
    scores[...] = lax.dot_general(
        query_ref[...], keys[...], (((1,), (1,)), ((), ())), preferred_element_type=jnp.float32
    ) * np.float32(HEAD**-0.5)

    def sending(at):
        return pltpu.make_async_copy(mass.at[pl.ds(at, SEL)], out.at[pl.ds(at, SEL)], out_sem)

    def soften(step, _):
        at = pl.multiple_of(step * SEL, SEL)
        part = jnp.where(place[...] <= column, scores[pl.ds(at, SEL)], -jnp.inf)
        part = jnp.exp(part - jnp.max(part, axis=1, keepdims=True))
        part = part * (1.0 / jnp.sum(part, axis=1, keepdims=True))
        mass[pl.ds(at, SEL)] = part.astype(jnp.bfloat16)
        sending(at).start()
        return 0

    lax.fori_loop(0, QPER, soften, 0)
    for head in range(QPER):
        sending(head * SEL).wait()


def mix_kernel(mass_ref, value_ref, past_ref, fresh_ref, out_ref, mass, values, sems):
    fetches = [pltpu.make_async_copy(value_ref, values.at[pl.ds(HIST, CONTEXT)], sems.at[QPER])]
    early = [
        pltpu.make_async_copy(past_ref.at[:, HEAD:], values.at[pl.ds(0, HIST)], sems.at[QPER + 1]),
        pltpu.make_async_copy(
            fresh_ref, values.at[pl.ds(HIST + CONTEXT, SEL)], sems.at[QPER + 1]
        ),
    ]
    for fetch in early:
        fetch.start()
    for head in range(QPER):
        rows = pl.ds(head * SEL, SEL)
        fetches.append(pltpu.make_async_copy(mass_ref.at[rows], mass.at[rows], sems.at[head]))
    for fetch in fetches:
        fetch.start()
    for fetch in early:
        fetch.wait()
    fetches[0].wait()
    for pair in range(0, QPER, 2):
        fetches[pair + 1].wait()
        fetches[pair + 2].wait()
        part = mass[pair * SEL : (pair + 2) * SEL]
        mixed = jnp.dot(part, values[...], preferred_element_type=jnp.float32)
        for head in range(2):
            at = (pair + head) * HEAD
            out_ref[:, at : at + HEAD] = mixed[head * SEL : (head + 1) * SEL].astype(jnp.bfloat16)


def per_device(hidden, w_query, w_key_value, block_kv, history_kv, block_lists, sel_pos, hist_len):
    z = lax.axis_index("z").reshape(1)
    sel = sel_pos[0]
    bf16, f32 = jnp.bfloat16, jnp.float32

    head = lax.axis_index("head").reshape(1)
    shapes = (256, WIDE), (NX, 2, 2, PIECE, HEAD), (NX, HALF, NZ * 256), (NH, HIST // NH, 256)
    both, pieces, rows, past = pl.pallas_call(
        prepare_kernel,
        out_shape=[jax.ShapeDtypeStruct(shape, bf16) for shape in shapes],
        in_specs=[SMEM] * 2 + [ANY] * 5,
        out_specs=[ANY] * 4,
        scratch_shapes=[pltpu.VMEM(shape, bf16) for shape in shapes]
        + [pltpu.SemaphoreType.DMA((8,))],
        compiler_params=PARAMS,
        cost_estimate=COST,
    )(z, head, hidden[0], w_query, w_key_value, block_kv, history_kv[0])

    pieces = lax.all_to_all(pieces, "x", 0, 0, tiled=True)
    w_up, w_down = [both], [both]
    for step in range(4):
        w_up.append(lax.ppermute(after(w_up[-1], w_down[max(step - 1, 0)]), "z", UP))
        if step < 3:
            w_down.append(lax.ppermute(after(w_down[-1], w_up[step]), "z", DOWN))
    received = lax.all_to_all(after(rows, pieces, w_up[1], w_down[1]), "x", 0, 0, tiled=True)
    received = after(received, w_up[3], w_down[3])
    swapped = lax.ppermute(received, "head", [(i, i ^ 1) for i in range(NH)])
    weights = w_down + w_up[:0:-1]
    partial = pl.pallas_call(
        project_kernel,
        out_shape=jax.ShapeDtypeStruct((NX, SEL, WIDE), f32),
        in_specs=[SMEM] + [ANY] * (NZ + 2),
        out_specs=ANY,
        scratch_shapes=[
            pltpu.VMEM((NZ * 256, WIDE), bf16),
            pltpu.VMEM((NX * SEL, NZ * 256), bf16),
            pltpu.VMEM((NX, SEL, WIDE), f32),
            pltpu.SemaphoreType.DMA((2,)),
        ],
        compiler_params=PARAMS,
        cost_estimate=COST,
    )(head, received, swapped, *weights)
    own = pieces.reshape(NX * 4, PIECE, HEAD)
    up, down = [own], [own]
    for step in range(4):
        before = up[step - 1] if step > 1 else w_up[3]
        down.append(lax.ppermute(after(down[-1], w_down[3], before), "z", DOWN))
        if step < 3:
            before = (down[step], partial) if step else (w_down[3],)
            up.append(lax.ppermute(after(up[-1], w_up[4], *before), "z", UP))
    held = down + up[:0:-1]

    partial = lax.all_to_all(partial, "x", 0, 0, tiled=True)
    past = lax.all_to_all(after(past, partial), "head", 0, 0, tiled=True).reshape(HIST, 2 * HEAD)
    column, inverse = sel.reshape(SEL, 1), jnp.asarray(INVERSE).reshape(1, HEAD)
    queries, fresh_keys, fresh_values = kernel_call(
        queries_kernel,
        [
            jax.ShapeDtypeStruct((QPER * SEL, HEAD), bf16),
            jax.ShapeDtypeStruct((SEL, HEAD), bf16),
            jax.ShapeDtypeStruct((SEL, HEAD), bf16),
        ],
        [hist_len, partial, column, inverse],
        smem=1,
    )

    raw = lax.all_to_all(pick(z, block_lists, held, 0), "x", 0, 0, tiled=True)
    mass = pl.pallas_call(
        weigh_kernel,
        out_shape=jax.ShapeDtypeStruct((QPER * SEL, KEYS), bf16),
        in_specs=[SMEM, VMEM, ANY] + [VMEM] * 5,
        out_specs=ANY,
        scratch_shapes=[
            pltpu.VMEM((CONTEXT, HEAD), bf16),
            pltpu.VMEM((KEYS, HEAD), bf16),
            pltpu.VMEM((1, KEYS), jnp.int32),
            pltpu.VMEM((QPER * SEL, KEYS), f32),
            pltpu.VMEM((QPER * SEL, KEYS), bf16),
            pltpu.SemaphoreType.DMA,
            pltpu.SemaphoreType.DMA,
        ],
        compiler_params=pltpu.CompilerParams(vmem_limit_bytes=56 << 20),
        cost_estimate=FREE,
    )(hist_len, queries, raw.reshape(CONTEXT, HEAD), past, fresh_keys, sel_pos, column, inverse)
    values = lax.all_to_all(pick(z, block_lists, held, 1), "x", 0, 0, tiled=True)
    values = values.reshape(CONTEXT, HEAD)
    mixed = pl.pallas_call(
        mix_kernel,
        out_shape=jax.ShapeDtypeStruct((SEL, QPER * HEAD), bf16),
        in_specs=[ANY] * 4,
        out_specs=VMEM,
        scratch_shapes=[
            pltpu.VMEM((QPER * SEL, KEYS), bf16),
            pltpu.VMEM((KEYS, HEAD), bf16),
            pltpu.SemaphoreType.DMA((QPER + 2,)),
        ],
        compiler_params=PARAMS,
        cost_estimate=FREE,
    )(mass, values, past, fresh_values)
    return mixed[None]


def solution(mesh):
    split = Mesh(mesh.devices.reshape(NZ, NX, NH), ("z", "x", "head"))
    store = ("z", "x")
    in_specs = (
        P(store, None, None),
        P(store, "head"),
        P(store, "head"),
        P(store, None, "head"),
        P(store, "head", None),
        P(),
        P(store, None),
        P(store),
    )
    return jax.shard_map(
        per_device, mesh=split, in_specs=in_specs, out_specs=P(store, None, "head"), check_vma=False
    )
```

```python
import functools

import jax
import jax.numpy as jnp
import numpy as np
from jax import lax
from jax.experimental import pallas as pl
from jax.experimental.pallas import tpu as pltpu
from jax.sharding import Mesh
from jax.sharding import PartitionSpec as P

NZ, NX, NH = 8, 4, 8
SEL, HEAD, QPER, BLOCK, RET, HIST = 128, 128, 4, 512, 8, 512
CONTEXT = RET * BLOCK
PIECE = BLOCK // NX
STEP = 4 * PIECE
WIDE = (QPER + 2) * HEAD
FAR = 1 << 20
FREE = pl.CostEstimate(flops=0, bytes_accessed=0, transcendentals=0)
COST = pl.CostEstimate(flops=5 * 10**10, bytes_accessed=1 << 20, transcendentals=0)
HALF = SEL // 2
KEYS = HIST + CONTEXT + SEL
INVERSE = (500000.0 ** (-(np.arange(64, dtype=np.float64) * 2.0 / 128))).astype(np.float32)
INVERSE = np.concatenate([INVERSE, INVERSE])
UP = [(i, (i + 1) % NZ) for i in range(NZ)]
DOWN = [(i, (i - 1) % NZ) for i in range(NZ)]
SMEM = pl.BlockSpec(memory_space=pltpu.SMEM)
VMEM = pl.BlockSpec(memory_space=pltpu.VMEM)
HBM = pl.BlockSpec(memory_space=pltpu.HBM)
ANY = pl.BlockSpec(memory_space=pl.ANY)


def grant(mebibytes):
    return pltpu.CompilerParams(vmem_limit_bytes=mebibytes << 20)


def kernel_call(body, out, inputs, smem=0, scratch=()):
    many = isinstance(out, (list, tuple))
    return pl.pallas_call(
        body,
        out_shape=out,
        in_specs=[SMEM] * smem + [VMEM] * (len(inputs) - smem),
        out_specs=[VMEM] * len(out) if many else VMEM,
        scratch_shapes=scratch,
        compiler_params=grant(16),
        cost_estimate=FREE,
    )(*inputs)


def after(value, *others):
    return lax.optimization_barrier((value, *others))[0]


def turn(values, cosine, sine):
    return values * cosine + pltpu.roll(values, 64, 1) * sine


def prepare_kernel(
    z_ref, head_ref, hidden, w_query, w_key_value, block, history,
    both, pieces, rows, past, held_both, held_pieces, held_rows, held_past, sems,
):
    loads = [
        [
            (w_query, held_both.at[:, : QPER * HEAD]),
            (w_key_value, held_both.at[:, QPER * HEAD :]),
        ],
        [],
        [],
        [(history.at[:, i * 256 : (i + 1) * 256], held_past.at[i]) for i in range(NH)],
    ]
    for x in range(NX):
        for kind in range(2):
            part = block.at[:, x * PIECE : (x + 1) * PIECE, kind * HEAD : (kind + 1) * HEAD]
            loads[1].append((part, held_pieces.at[x, kind]))
    mine = pl.ds(pl.multiple_of((head_ref[0] & 1) * HALF, HALF), HALF)
    for hop in range(NZ):
        chunk = ((z_ref[0] + hop) & (NZ - 1)) * NX
        for x in range(NX):
            at = pl.multiple_of((chunk + x) * 256, 256)
            to = held_rows.at[x, :, hop * 256 : (hop + 1) * 256]
            loads[2].append((hidden.at[mine, pl.ds(at, 256)], to))
    loads = [
        [pltpu.make_async_copy(*pair, sems.at[group]) for pair in pairs]
        for group, pairs in enumerate(loads)
    ]
    for group in loads:
        for load in group:
            load.start()
    stores = []
    pairs = (held_both, both), (held_pieces, pieces), (held_rows, rows), (held_past, past)
    for group, pair in enumerate(pairs):
        for load in loads[group]:
            load.wait()
        stores.append(pltpu.make_async_copy(*pair, sems.at[4 + group]))
        stores[-1].start()
    for store in stores:
        store.wait()


def waves(position, inverse):
    angle = position.astype(jnp.float32) * inverse
    turns = jnp.floor(angle * np.float32(2 / np.pi) + 0.5)
    rest = angle - turns * np.float32(1.5703125)
    rest = rest - turns * np.float32(4.837512969970703125e-4)
    rest = rest - turns * np.float32(7.54978995489188216e-8)
    square = rest * rest
    sine = np.float32(-1.9515295891e-4) * square + np.float32(8.3321608736e-3)
    sine = (sine * square + np.float32(-1.6666654611e-1)) * square * rest + rest
    cosine = np.float32(2.443315711809948e-5) * square + np.float32(-1.388731625493765e-3)
    cosine = (cosine * square + np.float32(4.166664568298827e-2)) * square * square
    cosine = cosine - np.float32(0.5) * square + np.float32(1.0)
    first = lax.broadcasted_iota(jnp.int32, angle.shape, 1) < 64
    quarter = turns.astype(jnp.int32) + jnp.where(first, 1, 0)
    wave = jnp.where((quarter & 1) == 1, cosine, sine)
    wave = jnp.where((quarter & 2) == 2, -wave, wave)
    other = pltpu.roll(wave, 64, 1)
    return jnp.where(first, wave, other), jnp.where(first, -other, wave)


def pick_kernel(kind, z_ref, lists_ref, *refs):
    sources, out, held, sems = refs[:NZ], *refs[NZ:]
    z = z_ref[0]

    def part(x):
        return pl.ds(x * RET, RET)

    def leaf(at, away, inner, low, high):
        if high - low == 1:
            to = held.at[at]
            pltpu.make_async_copy(sources[low].at[inner], to, sems.at[at >> 3]).start()
            return
        middle = (low + high) // 2

        @pl.when(away < middle)
        def _():
            leaf(at, away, inner, low, middle)

        @pl.when(away >= middle)
        def _():
            leaf(at, away, inner, middle, high)

    def one(at, _):
        block = lists_ref[z * NX + (at >> 3), at & 7]
        inner = ((block & 6) << 1) + 2 * kind + (block & 1)
        leaf(at, ((block >> 3) - z) & (NZ - 1), inner, 0, NZ)
        return 0

    lax.fori_loop(0, NX * RET, one, 0, unroll=8)
    stores = []
    for x in range(NX):
        pltpu.make_async_copy(held.at[part(x)], held.at[part(x)], sems.at[x]).wait()
        stores.append(pltpu.make_async_copy(held.at[part(x)], out.at[part(x)], sems.at[NX + x]))
        stores[-1].start()
    for store in stores:
        store.wait()


def pick(z, block_lists, sources, kind):
    out = pl.pallas_call(
        functools.partial(pick_kernel, kind),
        out_shape=jax.ShapeDtypeStruct((NX * RET, PIECE, HEAD), jnp.bfloat16),
        in_specs=[SMEM, SMEM] + [HBM] * NZ,
        out_specs=HBM,
        scratch_shapes=[
            pltpu.VMEM((NX * RET, PIECE, HEAD), jnp.bfloat16),
            pltpu.SemaphoreType.DMA((2 * NX,)),
        ],
        compiler_params=grant(56),
        cost_estimate=FREE,
    )(z, block_lists, *sources)
    return out.reshape(NX, RET, PIECE, HEAD)


def project_kernel(head_ref, received, swapped, *refs):
    weights, out, whole, rows, total, sems = refs[:NZ], *refs[NZ:]
    core = head_ref[0] & 1
    loads = [
        pltpu.make_async_copy(weights[hop], whole.at[pl.ds(hop * 256, 256)], sems.at[0])
        for hop in range(NZ)
    ]
    for x in range(NX):
        for source, half in ((received, core), (swapped, 1 - core)):
            at = pl.ds(pl.multiple_of(x * SEL + half * HALF, HALF), HALF)
            loads.append(pltpu.make_async_copy(source.at[x], rows.at[at], sems.at[0]))
    for load in loads:
        load.start()
    for load in loads:
        load.wait()
    stores = []
    for at in range(0, WIDE, 256):
        part = jnp.dot(rows[...], whole[:, at : at + 256], preferred_element_type=jnp.float32)
        total[:, :, at : at + 256] = part.reshape(NX, SEL, 256)
        columns = pl.ds(at, 256)
        stores.append(
            pltpu.make_async_copy(total.at[:, :, columns], out.at[:, :, columns], sems.at[1])
        )
        stores[-1].start()
    for store in stores:
        store.wait()


def queries_kernel(length_ref, partial_ref, column_ref, inverse_ref, query_ref, key_ref, value_ref):
    cosine, sine = waves(column_ref[...] + length_ref[0], inverse_ref[...])
    for part in range(QPER + 2):
        at = slice(part * HEAD, (part + 1) * HEAD)
        total = partial_ref[0, :, at] + partial_ref[1, :, at]
        total = total + partial_ref[2, :, at] + partial_ref[3, :, at]
        if part < QPER:
            query_ref[part * SEL : (part + 1) * SEL] = turn(total, cosine, sine).astype(jnp.bfloat16)
        elif part == QPER:
            fresh = total.astype(jnp.bfloat16).astype(jnp.float32)
            key_ref[...] = turn(fresh, cosine, sine).astype(jnp.bfloat16)
        else:
            value_ref[...] = total.astype(jnp.bfloat16)


def tables_kernel(
    length_ref, row_ref, column_ref, inverse_ref, out, place_ref, tables, sems
):
    length, inverse, column = length_ref[0], inverse_ref[...], column_ref[...]
    slots = lax.broadcasted_iota(jnp.int32, (1, HIST), 1)
    place_ref[:, :HIST] = jnp.where(slots < length, -1, FAR)
    place_ref[:, HIST + CONTEXT :] = row_ref[...]

    def sending(step):
        some = pl.ds(pl.multiple_of(step * STEP, STEP), STEP)
        return pltpu.make_async_copy(tables.at[:, some], out.at[:, some], sems.at[step])

    def one(step, _):
        rows = lax.broadcasted_iota(jnp.int32, (STEP, 1), 0)
        base = (step & 1) * (4 * BLOCK) + (step >> 1) * PIECE
        rows = base + (rows >> 7) * BLOCK + (rows & 127)
        at = pl.multiple_of(step * STEP, STEP)
        some = pl.ds(at, STEP)
        tables[0, some], tables[1, some] = waves(rows + length, inverse)
        sending(step).start()
        here = lax.broadcasted_iota(jnp.int32, (1, STEP), 1)
        here = base + (here >> 7) * BLOCK + (here & 127)
        hits = jnp.max(jnp.where(column == here, 1, 0), axis=0, keepdims=True)
        place_ref[:, pl.ds(at + HIST, STEP)] = jnp.where(hits > 0, FAR, here)
        return 0

    lax.fori_loop(0, CONTEXT // STEP, one, 0)
    for step in range(CONTEXT // STEP):
        sending(step).wait()


def weigh_kernel(
    query_ref, raw_ref, tables_ref, place_ref, past_ref, fresh_ref, column_ref,
    out, tables, keys, scores, mass, sems, sem,
):
    def fetching(step):
        some = pl.ds(pl.multiple_of(step * STEP, STEP), STEP)
        return pltpu.make_async_copy(tables_ref.at[:, some], tables.at[:, some], sems.at[step])

    for step in range(CONTEXT // STEP):
        fetching(step).start()
    keys[:HIST] = past_ref[:, :HEAD]
    keys[HIST + CONTEXT :] = fresh_ref[...]

    def rotate(step, _):
        at = pl.multiple_of(step * STEP, STEP)
        some = pl.ds(at, STEP)
        fetching(step).wait()
        key = turn(raw_ref[some].astype(jnp.float32), tables[0, some], tables[1, some])
        keys[pl.ds(at + HIST, STEP)] = key.astype(jnp.bfloat16)
        return 0

    lax.fori_loop(0, CONTEXT // STEP, rotate, 0)
    scores[...] = lax.dot_general(
        query_ref[...], keys[...], (((1,), (1,)), ((), ())), preferred_element_type=jnp.float32
    ) * np.float32(HEAD**-0.5)

    def sending(at):
        return pltpu.make_async_copy(mass.at[pl.ds(at, SEL)], out.at[pl.ds(at, SEL)], sem)

    def soften(step, _):
        at = pl.multiple_of(step * SEL, SEL)
        part = jnp.where(place_ref[...] <= column_ref[...], scores[pl.ds(at, SEL)], -jnp.inf)
        part = jnp.exp(part - jnp.max(part, axis=1, keepdims=True))
        part = part * (1.0 / jnp.sum(part, axis=1, keepdims=True))
        mass[pl.ds(at, SEL)] = part.astype(jnp.bfloat16)
        sending(at).start()
        return 0

    lax.fori_loop(0, QPER, soften, 0)
    for head in range(QPER):
        sending(head * SEL).wait()


def mix_kernel(mass_ref, value_ref, past_ref, fresh_ref, out_ref):
    late = HIST + CONTEXT
    mixed = jnp.dot(mass_ref[:, :HIST], past_ref[:, HEAD:], preferred_element_type=jnp.float32)
    mixed += jnp.dot(mass_ref[:, late:], fresh_ref[...], preferred_element_type=jnp.float32)
    mixed += jnp.dot(mass_ref[:, HIST:late], value_ref[...], preferred_element_type=jnp.float32)
    for head in range(QPER):
        part = mixed[head * SEL : (head + 1) * SEL]
        out_ref[:, head * HEAD : (head + 1) * HEAD] = part.astype(jnp.bfloat16)


def per_device(hidden, w_query, w_key_value, block_kv, history_kv, block_lists, sel_pos, hist_len):
    z = lax.axis_index("z").reshape(1)
    column, inverse = sel_pos[0].reshape(SEL, 1), jnp.asarray(INVERSE).reshape(1, HEAD)
    bf16, f32 = jnp.bfloat16, jnp.float32

    head = lax.axis_index("head").reshape(1)
    shapes = (256, WIDE), (NX, 2, 2, PIECE, HEAD), (NX, HALF, NZ * 256), (NH, HIST // NH, 256)
    both, pieces, rows, past = pl.pallas_call(
        prepare_kernel,
        out_shape=[jax.ShapeDtypeStruct(shape, bf16) for shape in shapes],
        in_specs=[SMEM] * 2 + [HBM] * 5,
        out_specs=[HBM] * 4,
        scratch_shapes=[pltpu.VMEM(shape, bf16) for shape in shapes]
        + [pltpu.SemaphoreType.DMA((8,))],
        compiler_params=grant(56),
        cost_estimate=COST,
    )(z, head, hidden[0], w_query, w_key_value, block_kv, history_kv[0])

    pieces = lax.all_to_all(pieces, "x", 0, 0, tiled=True)
    w_up, w_down = [both], [both]
    for step in range(4):
        w_up.append(lax.ppermute(after(w_up[-1], w_down[max(step - 1, 0)]), "z", UP))
        if step < 3:
            w_down.append(lax.ppermute(after(w_down[-1], w_up[step]), "z", DOWN))
    received = lax.all_to_all(after(rows, pieces, w_up[1], w_down[1]), "x", 0, 0, tiled=True)
    past = lax.all_to_all(after(past, received), "head", 0, 0, tiled=True).reshape(HIST, 2 * HEAD)
    received = after(received, w_up[3], w_down[3])
    swapped = lax.ppermute(received, "head", [(i, i ^ 1) for i in range(NH)])
    weights = w_down + w_up[:0:-1]
    own = pieces.reshape(NX * 4, PIECE, HEAD)
    up, down = [own], [own]
    for step in range(2):
        down.append(lax.ppermute(after(down[-1], w_down[3], w_up[3]), "z", DOWN))
        if step == 0:
            up.append(lax.ppermute(after(up[-1], w_up[4], w_down[3], past), "z", UP))

    partial = pl.pallas_call(
        project_kernel,
        out_shape=jax.ShapeDtypeStruct((NX, SEL, WIDE), f32),
        in_specs=[SMEM] + [ANY] * 2 + [HBM] * NZ,
        out_specs=HBM,
        scratch_shapes=[
            pltpu.VMEM((NZ * 256, WIDE), bf16),
            pltpu.VMEM((NX * SEL, NZ * 256), bf16),
            pltpu.VMEM((NX, SEL, WIDE), f32),
            pltpu.SemaphoreType.DMA((2,)),
        ],
        compiler_params=grant(56),
        cost_estimate=COST,
    )(head, after(received, past), swapped, *weights)
    up.append(lax.ppermute(after(up[1], down[1], partial), "z", UP))
    up.append(lax.ppermute(after(up[2], down[2]), "z", UP))
    down.append(lax.ppermute(after(down[2], up[1]), "z", DOWN))
    tables, place = pl.pallas_call(
        tables_kernel,
        out_shape=[
            jax.ShapeDtypeStruct((2, CONTEXT, HEAD), f32),
            jax.ShapeDtypeStruct((1, KEYS), jnp.int32),
        ],
        in_specs=[SMEM] + [VMEM] * 3,
        out_specs=[HBM, VMEM],
        scratch_shapes=[
            pltpu.VMEM((2, CONTEXT, HEAD), f32),
            pltpu.SemaphoreType.DMA((CONTEXT // STEP,)),
        ],
        compiler_params=grant(56),
        cost_estimate=FREE,
    )(after(hist_len, down[2]), sel_pos, column, inverse)
    down.append(lax.ppermute(after(down[3], up[2], place), "z", DOWN))
    held = down + up[:0:-1]
    partial = lax.all_to_all(partial, "x", 0, 0, tiled=True)
    queries, fresh_keys, fresh_values = kernel_call(
        queries_kernel,
        [
            jax.ShapeDtypeStruct((QPER * SEL, HEAD), bf16),
            jax.ShapeDtypeStruct((SEL, HEAD), bf16),
            jax.ShapeDtypeStruct((SEL, HEAD), bf16),
        ],
        [hist_len, partial, column, inverse],
        smem=1,
    )

    raw = lax.all_to_all(pick(z, block_lists, held, 0), "x", 0, 0, tiled=True)
    mass = pl.pallas_call(
        weigh_kernel,
        out_shape=jax.ShapeDtypeStruct((QPER * SEL, KEYS), bf16),
        in_specs=[VMEM] * 2 + [HBM] + [VMEM] * 4,
        out_specs=HBM,
        scratch_shapes=[
            pltpu.VMEM((2, CONTEXT, HEAD), f32),
            pltpu.VMEM((KEYS, HEAD), bf16),
            pltpu.VMEM((QPER * SEL, KEYS), f32),
            pltpu.VMEM((QPER * SEL, KEYS), bf16),
            pltpu.SemaphoreType.DMA((CONTEXT // STEP,)),
            pltpu.SemaphoreType.DMA,
        ],
        compiler_params=grant(56),
        cost_estimate=FREE,
    )(queries, raw.reshape(CONTEXT, HEAD), tables, place, past, fresh_keys, column)
    values = lax.all_to_all(pick(after(z, queries), block_lists, held, 1), "x", 0, 0, tiled=True)
    mixed = kernel_call(
        mix_kernel,
        jax.ShapeDtypeStruct((SEL, QPER * HEAD), bf16),
        [mass, values.reshape(CONTEXT, HEAD), past, fresh_values],
    )
    return mixed[None]


def solution(mesh):
    split = Mesh(mesh.devices.reshape(NZ, NX, NH), ("z", "x", "head"))
    store = ("z", "x")
    in_specs = (
        P(store, None, None),
        P(store, "head"),
        P(store, "head"),
        P(store, None, "head"),
        P(store, "head", None),
        P(),
        P(store, None),
        P(store),
    )
    return jax.shard_map(
        per_device, mesh=split, in_specs=in_specs, out_specs=P(store, None, "head"), check_vma=False
    )
```

```python
import functools

import jax
import jax.numpy as jnp
import numpy as np
from jax import lax
from jax.experimental import pallas as pl
from jax.experimental.pallas import tpu as pltpu
from jax.sharding import Mesh
from jax.sharding import PartitionSpec as P

NZ, NX, NH = 8, 4, 8
SEL, HEAD, QPER, BLOCK, RET, HIST = 128, 128, 4, 512, 8, 512
CONTEXT = RET * BLOCK
PIECE = BLOCK // NX
STEP = 4 * PIECE
WIDE = (QPER + 2) * HEAD
FAR = 1 << 20
FREE = pl.CostEstimate(flops=0, bytes_accessed=0, transcendentals=0)
COST = pl.CostEstimate(flops=5 * 10**10, bytes_accessed=1 << 20, transcendentals=0)
HALF = SEL // 2
KEYS = HIST + CONTEXT + SEL
INVERSE = (500000.0 ** (-(np.arange(64, dtype=np.float64) * 2.0 / 128))).astype(np.float32)
INVERSE = np.concatenate([INVERSE, INVERSE])
UP = [(i, (i + 1) % NZ) for i in range(NZ)]
DOWN = [(i, (i - 1) % NZ) for i in range(NZ)]
SMEM = pl.BlockSpec(memory_space=pltpu.SMEM)
VMEM = pl.BlockSpec(memory_space=pltpu.VMEM)
HBM = pl.BlockSpec(memory_space=pltpu.HBM)
ANY = pl.BlockSpec(memory_space=pl.ANY)


def grant(mebibytes):
    return pltpu.CompilerParams(vmem_limit_bytes=mebibytes << 20)


def kernel_call(body, out, inputs, smem=0, scratch=()):
    many = isinstance(out, (list, tuple))
    return pl.pallas_call(
        body,
        out_shape=out,
        in_specs=[SMEM] * smem + [VMEM] * (len(inputs) - smem),
        out_specs=[VMEM] * len(out) if many else VMEM,
        scratch_shapes=scratch,
        compiler_params=grant(16),
        cost_estimate=FREE,
    )(*inputs)


def after(value, *others):
    return lax.optimization_barrier((value, *others))[0]


def turn(values, cosine, sine):
    return values * cosine + pltpu.roll(values, 64, 1) * sine


def pack_kernel(w_query, w_key_value, both, held, sem):
    at = QPER * HEAD
    loads = [
        pltpu.make_async_copy(w_query, held.at[:, :at], sem),
        pltpu.make_async_copy(w_key_value, held.at[:, at:], sem),
    ]
    for load in loads:
        load.start()
    for load in loads:
        load.wait()
    store = pltpu.make_async_copy(held, both, sem)
    store.start()
    store.wait()


def prepare_kernel(
    z_ref, head_ref, hidden, block, history,
    pieces, rows, past, held_pieces, held_rows, held_past, sems,
):
    loads = [
        [],
        [],
        [(history.at[:, i * 256 : (i + 1) * 256], held_past.at[i]) for i in range(NH)],
    ]
    for x in range(NX):
        for kind in range(2):
            part = block.at[:, x * PIECE : (x + 1) * PIECE, kind * HEAD : (kind + 1) * HEAD]
            loads[0].append((part, held_pieces.at[x, kind]))
    mine = pl.ds(pl.multiple_of((head_ref[0] & 1) * HALF, HALF), HALF)
    for hop in range(NZ):
        chunk = ((z_ref[0] + hop) & (NZ - 1)) * NX
        for x in range(NX):
            at = pl.multiple_of((chunk + x) * 256, 256)
            to = held_rows.at[x, :, hop * 256 : (hop + 1) * 256]
            loads[1].append((hidden.at[mine, pl.ds(at, 256)], to))
    loads = [
        [pltpu.make_async_copy(*pair, sems.at[group]) for pair in pairs]
        for group, pairs in enumerate(loads)
    ]
    for group in loads:
        for load in group:
            load.start()
    stores = []
    pairs = (held_pieces, pieces), (held_rows, rows), (held_past, past)
    for group, pair in enumerate(pairs):
        for load in loads[group]:
            load.wait()
        stores.append(pltpu.make_async_copy(*pair, sems.at[3 + group]))
        stores[-1].start()
    for store in stores:
        store.wait()


def waves(position, inverse):
    angle = position.astype(jnp.float32) * inverse
    turns = jnp.floor(angle * np.float32(2 / np.pi) + 0.5)
    rest = angle - turns * np.float32(1.5703125)
    rest = rest - turns * np.float32(4.837512969970703125e-4)
    rest = rest - turns * np.float32(7.54978995489188216e-8)
    square = rest * rest
    sine = np.float32(-1.9515295891e-4) * square + np.float32(8.3321608736e-3)
    sine = (sine * square + np.float32(-1.6666654611e-1)) * square * rest + rest
    cosine = np.float32(2.443315711809948e-5) * square + np.float32(-1.388731625493765e-3)
    cosine = (cosine * square + np.float32(4.166664568298827e-2)) * square * square
    cosine = cosine - np.float32(0.5) * square + np.float32(1.0)
    first = lax.broadcasted_iota(jnp.int32, angle.shape, 1) < 64
    quarter = turns.astype(jnp.int32) + jnp.where(first, 1, 0)
    wave = jnp.where((quarter & 1) == 1, cosine, sine)
    wave = jnp.where((quarter & 2) == 2, -wave, wave)
    other = pltpu.roll(wave, 64, 1)
    return jnp.where(first, wave, other), jnp.where(first, -other, wave)


def pick_kernel(kind, z_ref, lists_ref, *refs):
    sources, out, sem = refs[:NZ], *refs[NZ:]
    z = z_ref[0]

    def leaf(at, away, inner, low, high):
        if high - low == 1:
            pltpu.make_async_copy(sources[low].at[inner], out.at[at], sem).start()
            return
        middle = (low + high) // 2

        @pl.when(away < middle)
        def _():
            leaf(at, away, inner, low, middle)

        @pl.when(away >= middle)
        def _():
            leaf(at, away, inner, middle, high)

    def one(at, _):
        block = lists_ref[z * NX + (at >> 3), at & 7]
        inner = ((block & 6) << 1) + 2 * kind + (block & 1)
        leaf(at, ((block >> 3) - z) & (NZ - 1), inner, 0, NZ)
        return 0

    lax.fori_loop(0, NX * RET, one, 0, unroll=4)
    pltpu.make_async_copy(out, out, sem).wait()


def pick(z, block_lists, sources, kind):
    out = pl.pallas_call(
        functools.partial(pick_kernel, kind),
        out_shape=jax.ShapeDtypeStruct((NX * RET, PIECE, HEAD), jnp.bfloat16),
        in_specs=[SMEM, SMEM] + [VMEM] * NZ,
        out_specs=HBM,
        scratch_shapes=[pltpu.SemaphoreType.DMA],
        compiler_params=grant(8),
        cost_estimate=FREE,
    )(z, block_lists, *sources)
    return out.reshape(NX, RET, PIECE, HEAD)


def project_kernel(head_ref, received, swapped, *refs):
    weights, out, whole, rows, total, sems = refs[:NZ], *refs[NZ:]
    core = head_ref[0] & 1
    loads = [
        pltpu.make_async_copy(weights[hop], whole.at[pl.ds(hop * 256, 256)], sems.at[0])
        for hop in range(NZ)
    ]
    for x in range(NX):
        for source, half in ((received, core), (swapped, 1 - core)):
            at = pl.ds(pl.multiple_of(x * SEL + half * HALF, HALF), HALF)
            loads.append(pltpu.make_async_copy(source.at[x], rows.at[at], sems.at[0]))
    for load in loads:
        load.start()
    for load in loads:
        load.wait()
    stores = []
    for at in range(0, WIDE, 256):
        part = jnp.dot(rows[...], whole[:, at : at + 256], preferred_element_type=jnp.float32)
        total[:, :, at : at + 256] = part.reshape(NX, SEL, 256)
        columns = pl.ds(at, 256)
        stores.append(
            pltpu.make_async_copy(total.at[:, :, columns], out.at[:, :, columns], sems.at[1])
        )
        stores[-1].start()
    for store in stores:
        store.wait()


def queries_kernel(length_ref, partial_ref, column_ref, inverse_ref, query_ref, key_ref, value_ref):
    cosine, sine = waves(column_ref[...] + length_ref[0], inverse_ref[...])
    for part in range(QPER + 2):
        at = slice(part * HEAD, (part + 1) * HEAD)
        total = partial_ref[0, :, at] + partial_ref[1, :, at]
        total = total + partial_ref[2, :, at] + partial_ref[3, :, at]
        if part < QPER:
            query_ref[part * SEL : (part + 1) * SEL] = turn(total, cosine, sine).astype(jnp.bfloat16)
        elif part == QPER:
            fresh = total.astype(jnp.bfloat16).astype(jnp.float32)
            key_ref[...] = turn(fresh, cosine, sine).astype(jnp.bfloat16)
        else:
            value_ref[...] = total.astype(jnp.bfloat16)


def tables_kernel(
    length_ref, row_ref, column_ref, inverse_ref, out, place_ref, tables, sems
):
    length, inverse, column = length_ref[0], inverse_ref[...], column_ref[...]
    slots = lax.broadcasted_iota(jnp.int32, (1, HIST), 1)
    place_ref[:, :HIST] = jnp.where(slots < length, -1, FAR)
    place_ref[:, HIST + CONTEXT :] = row_ref[...]

    def sending(step):
        some = pl.ds(pl.multiple_of(step * STEP, STEP), STEP)
        return pltpu.make_async_copy(tables.at[:, some], out.at[:, some], sems.at[step])

    def one(step, _):
        rows = lax.broadcasted_iota(jnp.int32, (STEP, 1), 0)
        base = (step & 1) * (4 * BLOCK) + (step >> 1) * PIECE
        rows = base + (rows >> 7) * BLOCK + (rows & 127)
        at = pl.multiple_of(step * STEP, STEP)
        some = pl.ds(at, STEP)
        tables[0, some], tables[1, some] = waves(rows + length, inverse)
        sending(step).start()
        here = lax.broadcasted_iota(jnp.int32, (1, STEP), 1)
        here = base + (here >> 7) * BLOCK + (here & 127)
        hits = jnp.max(jnp.where(column == here, 1, 0), axis=0, keepdims=True)
        place_ref[:, pl.ds(at + HIST, STEP)] = jnp.where(hits > 0, FAR, here)
        return 0

    lax.fori_loop(0, CONTEXT // STEP, one, 0)
    for step in range(CONTEXT // STEP):
        sending(step).wait()


def weigh_kernel(
    query_ref, raw_ref, tables_ref, place_ref, past_ref, fresh_ref, column_ref,
    out, tables, keys, scores, mass, sems, sem,
):
    def fetching(step):
        some = pl.ds(pl.multiple_of(step * STEP, STEP), STEP)
        return pltpu.make_async_copy(tables_ref.at[:, some], tables.at[:, some], sems.at[step])

    for step in range(CONTEXT // STEP):
        fetching(step).start()
    keys[:HIST] = past_ref[:, :HEAD]
    keys[HIST + CONTEXT :] = fresh_ref[...]

    def rotate(step, _):
        at = pl.multiple_of(step * STEP, STEP)
        some = pl.ds(at, STEP)
        fetching(step).wait()
        key = turn(raw_ref[some].astype(jnp.float32), tables[0, some], tables[1, some])
        keys[pl.ds(at + HIST, STEP)] = key.astype(jnp.bfloat16)
        return 0

    lax.fori_loop(0, CONTEXT // STEP, rotate, 0)
    scores[...] = lax.dot_general(
        query_ref[...], keys[...], (((1,), (1,)), ((), ())), preferred_element_type=jnp.float32
    ) * np.float32(HEAD**-0.5)

    def sending(at):
        return pltpu.make_async_copy(mass.at[pl.ds(at, SEL)], out.at[pl.ds(at, SEL)], sem)

    def soften(step, _):
        at = pl.multiple_of(step * SEL, SEL)
        part = jnp.where(place_ref[...] <= column_ref[...], scores[pl.ds(at, SEL)], -jnp.inf)
        part = jnp.exp(part - jnp.max(part, axis=1, keepdims=True))
        part = part * (1.0 / jnp.sum(part, axis=1, keepdims=True))
        mass[pl.ds(at, SEL)] = part.astype(jnp.bfloat16)
        sending(at).start()
        return 0

    lax.fori_loop(0, QPER, soften, 0)
    for head in range(QPER):
        sending(head * SEL).wait()


def mix_kernel(mass_ref, value_ref, past_ref, fresh_ref, out_ref):
    late = HIST + CONTEXT
    mixed = jnp.dot(mass_ref[:, :HIST], past_ref[:, HEAD:], preferred_element_type=jnp.float32)
    mixed += jnp.dot(mass_ref[:, late:], fresh_ref[...], preferred_element_type=jnp.float32)
    mixed += jnp.dot(mass_ref[:, HIST:late], value_ref[...], preferred_element_type=jnp.float32)
    for head in range(QPER):
        part = mixed[head * SEL : (head + 1) * SEL]
        out_ref[:, head * HEAD : (head + 1) * HEAD] = part.astype(jnp.bfloat16)


def per_device(hidden, w_query, w_key_value, block_kv, history_kv, block_lists, sel_pos, hist_len):
    z = lax.axis_index("z").reshape(1)
    column, inverse = sel_pos[0].reshape(SEL, 1), jnp.asarray(INVERSE).reshape(1, HEAD)
    bf16, f32 = jnp.bfloat16, jnp.float32

    head = lax.axis_index("head").reshape(1)
    both = pl.pallas_call(
        pack_kernel,
        out_shape=jax.ShapeDtypeStruct((256, WIDE), bf16),
        in_specs=[HBM] * 2,
        out_specs=HBM,
        scratch_shapes=[pltpu.VMEM((256, WIDE), bf16), pltpu.SemaphoreType.DMA],
        compiler_params=grant(56),
        cost_estimate=FREE,
    )(w_query, w_key_value)
    shapes = (NX, 2, 2, PIECE, HEAD), (NX, HALF, NZ * 256), (NH, HIST // NH, 256)
    pieces, rows, past = pl.pallas_call(
        prepare_kernel,
        out_shape=[jax.ShapeDtypeStruct(shape, bf16) for shape in shapes],
        in_specs=[SMEM] * 2 + [HBM] * 3,
        out_specs=[HBM] * 3,
        scratch_shapes=[pltpu.VMEM(shape, bf16) for shape in shapes]
        + [pltpu.SemaphoreType.DMA((6,))],
        compiler_params=grant(56),
        cost_estimate=COST,
    )(z, head, after(hidden[0], both), block_kv, history_kv[0])

    pieces = lax.all_to_all(pieces, "x", 0, 0, tiled=True)
    own = pieces.reshape(NX * 4, PIECE, HEAD)
    w_up, w_down, up, down = [both], [both], [own], [own]
    for step in range(3):
        w_down.append(lax.ppermute(after(w_down[-1], w_up[step]), "z", DOWN))
        w_up.append(lax.ppermute(after(w_up[-1], w_down[max(step - 1, 0)]), "z", UP))
    down.append(lax.ppermute(after(own, w_down[3], w_up[3]), "z", DOWN))
    w_up.append(lax.ppermute(after(w_up[3], w_down[2]), "z", UP))
    received = lax.all_to_all(after(rows, pieces, w_up[1], w_down[1]), "x", 0, 0, tiled=True)
    past = lax.all_to_all(after(past, received), "head", 0, 0, tiled=True).reshape(HIST, 2 * HEAD)
    received = after(received, w_up[3], w_down[3])
    swapped = lax.ppermute(received, "head", [(i, i ^ 1) for i in range(NH)])
    weights = w_down + w_up[:0:-1]
    down.append(lax.ppermute(after(down[1], w_down[3], w_up[3]), "z", DOWN))
    up.append(lax.ppermute(after(own, w_up[4], w_down[3], past), "z", UP))

    partial = pl.pallas_call(
        project_kernel,
        out_shape=jax.ShapeDtypeStruct((NX, SEL, WIDE), f32),
        in_specs=[SMEM] + [ANY] * 2 + [HBM] * NZ,
        out_specs=HBM,
        scratch_shapes=[
            pltpu.VMEM((NZ * 256, WIDE), bf16),
            pltpu.VMEM((NX * SEL, NZ * 256), bf16),
            pltpu.VMEM((NX, SEL, WIDE), f32),
            pltpu.SemaphoreType.DMA((2,)),
        ],
        compiler_params=grant(56),
        cost_estimate=COST,
    )(head, after(received, past), swapped, *weights)
    up.append(lax.ppermute(after(up[1], down[1], partial), "z", UP))
    up.append(lax.ppermute(after(up[2], down[2]), "z", UP))
    down.append(lax.ppermute(after(down[2], up[1]), "z", DOWN))
    tables, place = pl.pallas_call(
        tables_kernel,
        out_shape=[
            jax.ShapeDtypeStruct((2, CONTEXT, HEAD), f32),
            jax.ShapeDtypeStruct((1, KEYS), jnp.int32),
        ],
        in_specs=[SMEM] + [VMEM] * 3,
        out_specs=[HBM, VMEM],
        scratch_shapes=[
            pltpu.VMEM((2, CONTEXT, HEAD), f32),
            pltpu.SemaphoreType.DMA((CONTEXT // STEP,)),
        ],
        compiler_params=grant(16),
        cost_estimate=FREE,
    )(after(hist_len, down[2]), sel_pos, column, inverse)
    down.append(lax.ppermute(after(down[3], up[2], place), "z", DOWN))
    held = down + up[:0:-1]
    partial = lax.all_to_all(partial, "x", 0, 0, tiled=True)
    queries, fresh_keys, fresh_values = kernel_call(
        queries_kernel,
        [
            jax.ShapeDtypeStruct((QPER * SEL, HEAD), bf16),
            jax.ShapeDtypeStruct((SEL, HEAD), bf16),
            jax.ShapeDtypeStruct((SEL, HEAD), bf16),
        ],
        [hist_len, partial, column, inverse],
        smem=1,
    )

    raw = lax.all_to_all(pick(z, block_lists, held, 0), "x", 0, 0, tiled=True)
    mass = pl.pallas_call(
        weigh_kernel,
        out_shape=jax.ShapeDtypeStruct((QPER * SEL, KEYS), bf16),
        in_specs=[VMEM] * 2 + [HBM] + [VMEM] * 4,
        out_specs=HBM,
        scratch_shapes=[
            pltpu.VMEM((2, CONTEXT, HEAD), f32),
            pltpu.VMEM((KEYS, HEAD), bf16),
            pltpu.VMEM((QPER * SEL, KEYS), f32),
            pltpu.VMEM((QPER * SEL, KEYS), bf16),
            pltpu.SemaphoreType.DMA((CONTEXT // STEP,)),
            pltpu.SemaphoreType.DMA,
        ],
        compiler_params=grant(56),
        cost_estimate=FREE,
    )(queries, raw.reshape(CONTEXT, HEAD), tables, place, past, fresh_keys, column)
    values = lax.all_to_all(pick(after(z, queries), block_lists, held, 1), "x", 0, 0, tiled=True)
    mixed = kernel_call(
        mix_kernel,
        jax.ShapeDtypeStruct((SEL, QPER * HEAD), bf16),
        [mass, values.reshape(CONTEXT, HEAD), past, fresh_values],
    )
    return mixed[None]


def solution(mesh):
    split = Mesh(mesh.devices.reshape(NZ, NX, NH), ("z", "x", "head"))
    store = ("z", "x")
    in_specs = (
        P(store, None, None),
        P(store, "head"),
        P(store, "head"),
        P(store, None, "head"),
        P(store, "head", None),
        P(),
        P(store, None),
        P(store),
    )
    return jax.shard_map(
        per_device, mesh=split, in_specs=in_specs, out_specs=P(store, None, "head"), check_vma=False
    )
```

```python
import functools

import jax
import jax.numpy as jnp
import numpy as np
from jax import lax
from jax.experimental import pallas as pl
from jax.experimental.pallas import tpu as pltpu
from jax.sharding import Mesh
from jax.sharding import PartitionSpec as P

NZ, NX, NH = 8, 4, 8
SEL, HEAD, QPER, BLOCK, RET, HIST = 128, 128, 4, 512, 8, 512
CONTEXT = RET * BLOCK
PIECE = BLOCK // NX
STEP = 4 * PIECE
WIDE = (QPER + 2) * HEAD
FAR = 1 << 20
FREE = pl.CostEstimate(flops=0, bytes_accessed=0, transcendentals=0)
COST = pl.CostEstimate(flops=5 * 10**10, bytes_accessed=1 << 20, transcendentals=0)
HALF = SEL // 2
KEYS = HIST + CONTEXT + SEL
INVERSE = (500000.0 ** (-(np.arange(64, dtype=np.float64) * 2.0 / 128))).astype(np.float32)
INVERSE = np.concatenate([INVERSE, INVERSE])
UP = [(i, (i + 1) % NZ) for i in range(NZ)]
DOWN = [(i, (i - 1) % NZ) for i in range(NZ)]
SMEM = pl.BlockSpec(memory_space=pltpu.SMEM)
VMEM = pl.BlockSpec(memory_space=pltpu.VMEM)
HBM = pl.BlockSpec(memory_space=pltpu.HBM)
ANY = pl.BlockSpec(memory_space=pl.ANY)


def grant(mebibytes):
    return pltpu.CompilerParams(vmem_limit_bytes=mebibytes << 20)


def kernel_call(body, out, inputs, smem=0, scratch=()):
    many = isinstance(out, (list, tuple))
    return pl.pallas_call(
        body,
        out_shape=out,
        in_specs=[SMEM] * smem + [VMEM] * (len(inputs) - smem),
        out_specs=[VMEM] * len(out) if many else VMEM,
        scratch_shapes=scratch,
        compiler_params=grant(16),
        cost_estimate=FREE,
    )(*inputs)


def after(value, *others):
    return lax.optimization_barrier((value, *others))[0]


def turn(values, cosine, sine):
    return values * cosine + pltpu.roll(values, 64, 1) * sine


def pack_kernel(w_query, w_key_value, both, held, sem):
    at = QPER * HEAD
    loads = [
        pltpu.make_async_copy(w_query, held.at[:, :at], sem),
        pltpu.make_async_copy(w_key_value, held.at[:, at:], sem),
    ]
    for load in loads:
        load.start()
    for load in loads:
        load.wait()
    store = pltpu.make_async_copy(held, both, sem)
    store.start()
    store.wait()


def prepare_kernel(
    z_ref, head_ref, hidden, block, history,
    pieces, rows, past, held_pieces, held_rows, held_past, sems,
):
    loads = [
        [],
        [],
        [(history.at[:, i * 256 : (i + 1) * 256], held_past.at[i]) for i in range(NH)],
    ]
    for x in range(NX):
        for kind in range(2):
            part = block.at[:, x * PIECE : (x + 1) * PIECE, kind * HEAD : (kind + 1) * HEAD]
            loads[0].append((part, held_pieces.at[x, kind]))
    mine = pl.ds(pl.multiple_of((head_ref[0] & 1) * HALF, HALF), HALF)
    for hop in range(NZ):
        chunk = ((z_ref[0] + hop) & (NZ - 1)) * NX
        for x in range(NX):
            at = pl.multiple_of((chunk + x) * 256, 256)
            to = held_rows.at[x, :, hop * 256 : (hop + 1) * 256]
            loads[1].append((hidden.at[mine, pl.ds(at, 256)], to))
    loads = [
        [pltpu.make_async_copy(*pair, sems.at[group]) for pair in pairs]
        for group, pairs in enumerate(loads)
    ]
    for group in loads:
        for load in group:
            load.start()
    stores = []
    pairs = (held_pieces, pieces), (held_rows, rows), (held_past, past)
    for group, pair in enumerate(pairs):
        for load in loads[group]:
            load.wait()
        stores.append(pltpu.make_async_copy(*pair, sems.at[3 + group]))
        stores[-1].start()
    for store in stores:
        store.wait()


def waves(position, inverse):
    angle = position.astype(jnp.float32) * inverse
    turns = jnp.floor(angle * np.float32(2 / np.pi) + 0.5)
    rest = angle - turns * np.float32(1.5703125)
    rest = rest - turns * np.float32(4.837512969970703125e-4)
    rest = rest - turns * np.float32(7.54978995489188216e-8)
    square = rest * rest
    sine = np.float32(-1.9515295891e-4) * square + np.float32(8.3321608736e-3)
    sine = (sine * square + np.float32(-1.6666654611e-1)) * square * rest + rest
    cosine = np.float32(2.443315711809948e-5) * square + np.float32(-1.388731625493765e-3)
    cosine = (cosine * square + np.float32(4.166664568298827e-2)) * square * square
    cosine = cosine - np.float32(0.5) * square + np.float32(1.0)
    first = lax.broadcasted_iota(jnp.int32, angle.shape, 1) < 64
    quarter = turns.astype(jnp.int32) + jnp.where(first, 1, 0)
    wave = jnp.where((quarter & 1) == 1, cosine, sine)
    wave = jnp.where((quarter & 2) == 2, -wave, wave)
    other = pltpu.roll(wave, 64, 1)
    return jnp.where(first, wave, other), jnp.where(first, -other, wave)


def pick_kernel(kind, z_ref, lists_ref, *refs):
    sources, out, sem = refs[:NZ], *refs[NZ:]
    z = z_ref[0]

    def leaf(at, away, inner, low, high):
        if high - low == 1:
            pltpu.make_async_copy(sources[low].at[inner], out.at[at], sem).start()
            return
        middle = (low + high) // 2

        @pl.when(away < middle)
        def _():
            leaf(at, away, inner, low, middle)

        @pl.when(away >= middle)
        def _():
            leaf(at, away, inner, middle, high)

    def one(at, _):
        block = lists_ref[z * NX + (at >> 3), at & 7]
        inner = ((block & 6) << 1) + 2 * kind + (block & 1)
        leaf(at, ((block >> 3) - z) & (NZ - 1), inner, 0, NZ)
        return 0

    lax.fori_loop(0, NX * RET, one, 0, unroll=4)
    pltpu.make_async_copy(out, out, sem).wait()


def pick(z, block_lists, sources, kind):
    out = pl.pallas_call(
        functools.partial(pick_kernel, kind),
        out_shape=jax.ShapeDtypeStruct((NX * RET, PIECE, HEAD), jnp.bfloat16),
        in_specs=[SMEM, SMEM] + [VMEM] * NZ,
        out_specs=HBM,
        scratch_shapes=[pltpu.SemaphoreType.DMA],
        compiler_params=grant(8),
        cost_estimate=FREE,
    )(z, block_lists, *sources)
    return out.reshape(NX, RET, PIECE, HEAD)


def project_kernel(head_ref, received, swapped, *refs):
    weights, out, whole, rows, total, sems = refs[:NZ], *refs[NZ:]
    core = head_ref[0] & 1
    loads = [
        pltpu.make_async_copy(weights[hop], whole.at[pl.ds(hop * 256, 256)], sems.at[0])
        for hop in range(NZ)
    ]
    for x in range(NX):
        for source, half in ((received, core), (swapped, 1 - core)):
            at = pl.ds(pl.multiple_of(x * SEL + half * HALF, HALF), HALF)
            loads.append(pltpu.make_async_copy(source.at[x], rows.at[at], sems.at[0]))
    for load in loads:
        load.start()
    for load in loads:
        load.wait()
    stores = []
    for at in range(0, WIDE, 256):
        part = jnp.dot(rows[...], whole[:, at : at + 256], preferred_element_type=jnp.float32)
        total[:, :, at : at + 256] = part.reshape(NX, SEL, 256)
        columns = pl.ds(at, 256)
        stores.append(
            pltpu.make_async_copy(total.at[:, :, columns], out.at[:, :, columns], sems.at[1])
        )
        stores[-1].start()
    for store in stores:
        store.wait()


def queries_kernel(length_ref, partial_ref, column_ref, inverse_ref, query_ref, key_ref, value_ref):
    cosine, sine = waves(column_ref[...] + length_ref[0], inverse_ref[...])
    for part in range(QPER + 2):
        at = slice(part * HEAD, (part + 1) * HEAD)
        total = partial_ref[0, :, at] + partial_ref[1, :, at]
        total = total + partial_ref[2, :, at] + partial_ref[3, :, at]
        if part < QPER:
            query_ref[part * SEL : (part + 1) * SEL] = turn(total, cosine, sine).astype(jnp.bfloat16)
        elif part == QPER:
            fresh = total.astype(jnp.bfloat16).astype(jnp.float32)
            key_ref[...] = turn(fresh, cosine, sine).astype(jnp.bfloat16)
        else:
            value_ref[...] = total.astype(jnp.bfloat16)


def tables_kernel(
    length_ref, row_ref, column_ref, inverse_ref, out, place_ref, tables, sems
):
    length, inverse, column = length_ref[0], inverse_ref[...], column_ref[...]
    slots = lax.broadcasted_iota(jnp.int32, (1, HIST), 1)
    place_ref[:, :HIST] = jnp.where(slots < length, -1, FAR)
    place_ref[:, HIST + CONTEXT :] = row_ref[...]

    def sending(step):
        some = pl.ds(pl.multiple_of(step * STEP, STEP), STEP)
        return pltpu.make_async_copy(tables.at[:, some], out.at[:, some], sems.at[step])

    def one(step, _):
        rows = lax.broadcasted_iota(jnp.int32, (STEP, 1), 0)
        base = (step & 1) * (4 * BLOCK) + (step >> 1) * PIECE
        rows = base + (rows >> 7) * BLOCK + (rows & 127)
        at = pl.multiple_of(step * STEP, STEP)
        some = pl.ds(at, STEP)
        tables[0, some], tables[1, some] = waves(rows + length, inverse)
        sending(step).start()
        here = lax.broadcasted_iota(jnp.int32, (1, STEP), 1)
        here = base + (here >> 7) * BLOCK + (here & 127)
        hits = jnp.max(jnp.where(column == here, 1, 0), axis=0, keepdims=True)
        place_ref[:, pl.ds(at + HIST, STEP)] = jnp.where(hits > 0, FAR, here)
        return 0

    lax.fori_loop(0, CONTEXT // STEP, one, 0)
    for step in range(CONTEXT // STEP):
        sending(step).wait()


def weigh_kernel(
    query_ref, raw_ref, tables_ref, place_ref, past_ref, fresh_ref, value_ref, column_ref,
    out, early_ref, tables, keys, scores, mass, sems, sem,
):
    def fetching(step):
        some = pl.ds(pl.multiple_of(step * STEP, STEP), STEP)
        return pltpu.make_async_copy(tables_ref.at[:, some], tables.at[:, some], sems.at[step])

    for step in range(CONTEXT // STEP):
        fetching(step).start()
    keys[:HIST] = past_ref[:, :HEAD]
    keys[HIST + CONTEXT :] = fresh_ref[...]

    def rotate(step, _):
        at = pl.multiple_of(step * STEP, STEP)
        some = pl.ds(at, STEP)
        fetching(step).wait()
        key = turn(raw_ref[some].astype(jnp.float32), tables[0, some], tables[1, some])
        keys[pl.ds(at + HIST, STEP)] = key.astype(jnp.bfloat16)
        return 0

    lax.fori_loop(0, CONTEXT // STEP, rotate, 0)
    scores[...] = lax.dot_general(
        query_ref[...], keys[...], (((1,), (1,)), ((), ())), preferred_element_type=jnp.float32
    ) * np.float32(HEAD**-0.5)

    def sending(at):
        return pltpu.make_async_copy(mass.at[pl.ds(at, SEL)], out.at[pl.ds(at, SEL)], sem)

    def soften(step, _):
        at = pl.multiple_of(step * SEL, SEL)
        part = jnp.where(place_ref[...] <= column_ref[...], scores[pl.ds(at, SEL)], -jnp.inf)
        part = jnp.exp(part - jnp.max(part, axis=1, keepdims=True))
        part = part * (1.0 / jnp.sum(part, axis=1, keepdims=True))
        part = part.astype(jnp.bfloat16)
        mass[pl.ds(at, SEL)] = part[:, HIST : HIST + CONTEXT]
        sending(at).start()
        early = jnp.dot(part[:, :HIST], past_ref[:, HEAD:], preferred_element_type=jnp.float32)
        early += jnp.dot(
            part[:, HIST + CONTEXT :], value_ref[...], preferred_element_type=jnp.float32
        )
        early_ref[pl.ds(at, SEL)] = early
        return 0

    lax.fori_loop(0, QPER, soften, 0)
    for head in range(QPER):
        sending(head * SEL).wait()


def mix_kernel(mass_ref, value_ref, early_ref, out_ref):
    mixed = early_ref[...] + jnp.dot(
        mass_ref[...], value_ref[...], preferred_element_type=jnp.float32
    )
    for head in range(QPER):
        part = mixed[head * SEL : (head + 1) * SEL]
        out_ref[:, head * HEAD : (head + 1) * HEAD] = part.astype(jnp.bfloat16)


def per_device(hidden, w_query, w_key_value, block_kv, history_kv, block_lists, sel_pos, hist_len):
    z = lax.axis_index("z").reshape(1)
    column, inverse = sel_pos[0].reshape(SEL, 1), jnp.asarray(INVERSE).reshape(1, HEAD)
    bf16, f32 = jnp.bfloat16, jnp.float32

    head = lax.axis_index("head").reshape(1)
    both = pl.pallas_call(
        pack_kernel,
        out_shape=jax.ShapeDtypeStruct((256, WIDE), bf16),
        in_specs=[HBM] * 2,
        out_specs=HBM,
        scratch_shapes=[pltpu.VMEM((256, WIDE), bf16), pltpu.SemaphoreType.DMA],
        compiler_params=grant(56),
        cost_estimate=FREE,
    )(w_query, w_key_value)
    shapes = (NX, 2, 2, PIECE, HEAD), (NX, HALF, NZ * 256), (NH, HIST // NH, 256)
    pieces, rows, past = pl.pallas_call(
        prepare_kernel,
        out_shape=[jax.ShapeDtypeStruct(shape, bf16) for shape in shapes],
        in_specs=[SMEM] * 2 + [HBM] * 3,
        out_specs=[HBM] * 3,
        scratch_shapes=[pltpu.VMEM(shape, bf16) for shape in shapes]
        + [pltpu.SemaphoreType.DMA((6,))],
        compiler_params=grant(56),
        cost_estimate=COST,
    )(z, head, after(hidden[0], both), block_kv, history_kv[0])

    pieces = lax.all_to_all(pieces, "x", 0, 0, tiled=True)
    own = pieces.reshape(NX * 4, PIECE, HEAD)
    w_up, w_down, up, down = [both], [both], [own], [own]
    for step in range(3):
        w_down.append(lax.ppermute(after(w_down[-1], w_up[step]), "z", DOWN))
        w_up.append(lax.ppermute(after(w_up[-1], w_down[max(step - 1, 0)]), "z", UP))
    down.append(lax.ppermute(after(own, w_down[3], w_up[3]), "z", DOWN))
    w_up.append(lax.ppermute(after(w_up[3], w_down[2]), "z", UP))
    received = lax.all_to_all(after(rows, pieces, w_up[1], w_down[1]), "x", 0, 0, tiled=True)
    past = lax.all_to_all(after(past, received), "head", 0, 0, tiled=True).reshape(HIST, 2 * HEAD)
    received = after(received, w_up[3], w_down[3])
    swapped = lax.ppermute(received, "head", [(i, i ^ 1) for i in range(NH)])
    weights = w_down + w_up[:0:-1]
    down.append(lax.ppermute(after(down[1], w_down[3], w_up[3]), "z", DOWN))
    up.append(lax.ppermute(after(own, w_up[4], w_down[3], past), "z", UP))

    partial = pl.pallas_call(
        project_kernel,
        out_shape=jax.ShapeDtypeStruct((NX, SEL, WIDE), f32),
        in_specs=[SMEM] + [ANY] * 2 + [HBM] * NZ,
        out_specs=HBM,
        scratch_shapes=[
            pltpu.VMEM((NZ * 256, WIDE), bf16),
            pltpu.VMEM((NX * SEL, NZ * 256), bf16),
            pltpu.VMEM((NX, SEL, WIDE), f32),
            pltpu.SemaphoreType.DMA((2,)),
        ],
        compiler_params=grant(56),
        cost_estimate=COST,
    )(head, after(received, past), swapped, *weights)
    up.append(lax.ppermute(after(up[1], down[1], partial), "z", UP))
    up.append(lax.ppermute(after(up[2], down[2]), "z", UP))
    down.append(lax.ppermute(after(down[2], up[1]), "z", DOWN))
    tables, place = pl.pallas_call(
        tables_kernel,
        out_shape=[
            jax.ShapeDtypeStruct((2, CONTEXT, HEAD), f32),
            jax.ShapeDtypeStruct((1, KEYS), jnp.int32),
        ],
        in_specs=[SMEM] + [VMEM] * 3,
        out_specs=[HBM, VMEM],
        scratch_shapes=[
            pltpu.VMEM((2, CONTEXT, HEAD), f32),
            pltpu.SemaphoreType.DMA((CONTEXT // STEP,)),
        ],
        compiler_params=grant(16),
        cost_estimate=FREE,
    )(after(hist_len, down[2]), sel_pos, column, inverse)
    down.append(lax.ppermute(after(down[3], up[2], place), "z", DOWN))
    held = down + up[:0:-1]
    partial = lax.all_to_all(partial, "x", 0, 0, tiled=True)
    queries, fresh_keys, fresh_values = kernel_call(
        queries_kernel,
        [
            jax.ShapeDtypeStruct((QPER * SEL, HEAD), bf16),
            jax.ShapeDtypeStruct((SEL, HEAD), bf16),
            jax.ShapeDtypeStruct((SEL, HEAD), bf16),
        ],
        [hist_len, partial, column, inverse],
        smem=1,
    )

    raw = lax.all_to_all(pick(z, block_lists, held, 0), "x", 0, 0, tiled=True)
    mass, early = pl.pallas_call(
        weigh_kernel,
        out_shape=[
            jax.ShapeDtypeStruct((QPER * SEL, CONTEXT), bf16),
            jax.ShapeDtypeStruct((QPER * SEL, HEAD), f32),
        ],
        in_specs=[VMEM] * 2 + [HBM] + [VMEM] * 5,
        out_specs=[HBM, VMEM],
        scratch_shapes=[
            pltpu.VMEM((2, CONTEXT, HEAD), f32),
            pltpu.VMEM((KEYS, HEAD), bf16),
            pltpu.VMEM((QPER * SEL, KEYS), f32),
            pltpu.VMEM((QPER * SEL, CONTEXT), bf16),
            pltpu.SemaphoreType.DMA((CONTEXT // STEP,)),
            pltpu.SemaphoreType.DMA,
        ],
        compiler_params=grant(56),
        cost_estimate=FREE,
    )(queries, raw.reshape(CONTEXT, HEAD), tables, place, past, fresh_keys, fresh_values, column)
    values = lax.all_to_all(pick(after(z, queries), block_lists, held, 1), "x", 0, 0, tiled=True)
    mixed = kernel_call(
        mix_kernel,
        jax.ShapeDtypeStruct((SEL, QPER * HEAD), bf16),
        [mass, values.reshape(CONTEXT, HEAD), early],
    )
    return mixed[None]


def solution(mesh):
    split = Mesh(mesh.devices.reshape(NZ, NX, NH), ("z", "x", "head"))
    store = ("z", "x")
    in_specs = (
        P(store, None, None),
        P(store, "head"),
        P(store, "head"),
        P(store, None, "head"),
        P(store, "head", None),
        P(),
        P(store, None),
        P(store),
    )
    return jax.shard_map(
        per_device, mesh=split, in_specs=in_specs, out_specs=P(store, None, "head"), check_vma=False
    )
```

```python
import functools

import jax
import jax.numpy as jnp
import numpy as np
from jax import lax
from jax.experimental import pallas as pl
from jax.experimental.pallas import tpu as pltpu
from jax.sharding import Mesh
from jax.sharding import PartitionSpec as P

NZ, NX, NH = 8, 4, 8
SEL, HEAD, QPER, BLOCK, RET, HIST = 128, 128, 4, 512, 8, 512
CONTEXT = RET * BLOCK
PIECE = BLOCK // NX
STEP = 4 * PIECE
WIDE = (QPER + 2) * HEAD
FAR = 1 << 20
FREE = pl.CostEstimate(flops=0, bytes_accessed=0, transcendentals=0)
COST = pl.CostEstimate(flops=5 * 10**10, bytes_accessed=1 << 20, transcendentals=0)
HALF = SEL // 2
KEYS = HIST + CONTEXT + SEL
INVERSE = (500000.0 ** (-(np.arange(64, dtype=np.float64) * 2.0 / 128))).astype(np.float32)
INVERSE = np.concatenate([INVERSE, INVERSE])
UP = [(i, (i + 1) % NZ) for i in range(NZ)]
DOWN = [(i, (i - 1) % NZ) for i in range(NZ)]
SMEM = pl.BlockSpec(memory_space=pltpu.SMEM)
VMEM = pl.BlockSpec(memory_space=pltpu.VMEM)
HBM = pl.BlockSpec(memory_space=pltpu.HBM)
ANY = pl.BlockSpec(memory_space=pl.ANY)


def grant(mebibytes):
    return pltpu.CompilerParams(vmem_limit_bytes=mebibytes << 20)


def kernel_call(body, out, inputs, smem=0, scratch=()):
    many = isinstance(out, (list, tuple))
    return pl.pallas_call(
        body,
        out_shape=out,
        in_specs=[SMEM] * smem + [VMEM] * (len(inputs) - smem),
        out_specs=[VMEM] * len(out) if many else VMEM,
        scratch_shapes=scratch,
        compiler_params=grant(16),
        cost_estimate=FREE,
    )(*inputs)


def after(value, *others):
    return lax.optimization_barrier((value, *others))[0]


def turn(values, cosine, sine):
    return values * cosine + pltpu.roll(values, 64, 1) * sine


def pack_kernel(w_query, w_key_value, both, held, sem):
    at = QPER * HEAD
    loads = [
        pltpu.make_async_copy(w_query, held.at[:, :at], sem),
        pltpu.make_async_copy(w_key_value, held.at[:, at:], sem),
    ]
    for load in loads:
        load.start()
    for load in loads:
        load.wait()
    store = pltpu.make_async_copy(held, both, sem)
    store.start()
    store.wait()


def prepare_kernel(
    z_ref, head_ref, hidden, block, history,
    pieces, rows, past, held_pieces, held_rows, held_past, sems,
):
    loads = [
        [],
        [],
        [(history.at[:, i * 256 : (i + 1) * 256], held_past.at[i]) for i in range(NH)],
    ]
    for x in range(NX):
        for kind in range(2):
            part = block.at[:, x * PIECE : (x + 1) * PIECE, kind * HEAD : (kind + 1) * HEAD]
            loads[0].append((part, held_pieces.at[x, kind]))
    mine = pl.ds(pl.multiple_of((head_ref[0] & 1) * HALF, HALF), HALF)
    for hop in range(NZ):
        chunk = ((z_ref[0] + hop) & (NZ - 1)) * NX
        for x in range(NX):
            at = pl.multiple_of((chunk + x) * 256, 256)
            to = held_rows.at[x, :, hop * 256 : (hop + 1) * 256]
            loads[1].append((hidden.at[mine, pl.ds(at, 256)], to))
    loads = [
        [pltpu.make_async_copy(*pair, sems.at[group]) for pair in pairs]
        for group, pairs in enumerate(loads)
    ]
    for group in loads:
        for load in group:
            load.start()
    stores = []
    pairs = (held_pieces, pieces), (held_rows, rows), (held_past, past)
    for group, pair in enumerate(pairs):
        for load in loads[group]:
            load.wait()
        stores.append(pltpu.make_async_copy(*pair, sems.at[3 + group]))
        stores[-1].start()
    for store in stores:
        store.wait()


def waves(position, inverse):
    angle = position.astype(jnp.float32) * inverse
    turns = jnp.floor(angle * np.float32(2 / np.pi) + 0.5)
    rest = angle - turns * np.float32(1.5703125)
    rest = rest - turns * np.float32(4.837512969970703125e-4)
    rest = rest - turns * np.float32(7.54978995489188216e-8)
    square = rest * rest
    sine = np.float32(-1.9515295891e-4) * square + np.float32(8.3321608736e-3)
    sine = (sine * square + np.float32(-1.6666654611e-1)) * square * rest + rest
    cosine = np.float32(2.443315711809948e-5) * square + np.float32(-1.388731625493765e-3)
    cosine = (cosine * square + np.float32(4.166664568298827e-2)) * square * square
    cosine = cosine - np.float32(0.5) * square + np.float32(1.0)
    first = lax.broadcasted_iota(jnp.int32, angle.shape, 1) < 64
    quarter = turns.astype(jnp.int32) + jnp.where(first, 1, 0)
    wave = jnp.where((quarter & 1) == 1, cosine, sine)
    wave = jnp.where((quarter & 2) == 2, -wave, wave)
    other = pltpu.roll(wave, 64, 1)
    return jnp.where(first, wave, other), jnp.where(first, -other, wave)


def pick_kernel(kind, z_ref, lists_ref, *refs):
    sources, out, sem = refs[:NZ], *refs[NZ:]
    z = z_ref[0]

    def leaf(at, away, inner, low, high):
        if high - low == 1:
            pltpu.make_async_copy(sources[low].at[inner], out.at[at], sem).start()
            return
        middle = (low + high) // 2

        @pl.when(away < middle)
        def _():
            leaf(at, away, inner, low, middle)

        @pl.when(away >= middle)
        def _():
            leaf(at, away, inner, middle, high)

    def one(at, _):
        block = lists_ref[z * NX + (at >> 3), at & 7]
        inner = ((block & 6) << 1) + 2 * kind + (block & 1)
        leaf(at, ((block >> 3) - z) & (NZ - 1), inner, 0, NZ)
        return 0

    lax.fori_loop(0, NX * RET, one, 0, unroll=4)
    pltpu.make_async_copy(out, out, sem).wait()


def pick(z, block_lists, sources, kind):
    out = pl.pallas_call(
        functools.partial(pick_kernel, kind),
        out_shape=jax.ShapeDtypeStruct((NX * RET, PIECE, HEAD), jnp.bfloat16),
        in_specs=[SMEM, SMEM] + [VMEM] * NZ,
        out_specs=HBM,
        scratch_shapes=[pltpu.SemaphoreType.DMA],
        compiler_params=grant(8),
        cost_estimate=FREE,
    )(z, block_lists, *sources)
    return out.reshape(NX, RET, PIECE, HEAD)


def project_kernel(head_ref, received, swapped, *refs):
    weights, out, whole, rows, total, sems = refs[:NZ], *refs[NZ:]
    core = head_ref[0] & 1
    loads = [
        pltpu.make_async_copy(weights[hop], whole.at[pl.ds(hop * 256, 256)], sems.at[0])
        for hop in range(NZ)
    ]
    for x in range(NX):
        for source, half in ((received, core), (swapped, 1 - core)):
            at = pl.ds(pl.multiple_of(x * SEL + half * HALF, HALF), HALF)
            loads.append(pltpu.make_async_copy(source.at[x], rows.at[at], sems.at[0]))
    for load in loads:
        load.start()
    for load in loads:
        load.wait()
    stores = []
    for at in range(0, WIDE, 256):
        part = jnp.dot(rows[...], whole[:, at : at + 256], preferred_element_type=jnp.float32)
        total[:, :, at : at + 256] = part.reshape(NX, SEL, 256)
        columns = pl.ds(at, 256)
        stores.append(
            pltpu.make_async_copy(total.at[:, :, columns], out.at[:, :, columns], sems.at[1])
        )
        stores[-1].start()
    for store in stores:
        store.wait()


def queries_kernel(length_ref, partial_ref, column_ref, inverse_ref, query_ref, key_ref, value_ref):
    cosine, sine = waves(column_ref[...] + length_ref[0], inverse_ref[...])
    for part in range(QPER + 2):
        at = slice(part * HEAD, (part + 1) * HEAD)
        total = partial_ref[0, :, at] + partial_ref[1, :, at]
        total = total + partial_ref[2, :, at] + partial_ref[3, :, at]
        if part < QPER:
            query_ref[part * SEL : (part + 1) * SEL] = turn(total, cosine, sine).astype(jnp.bfloat16)
        elif part == QPER:
            fresh = total.astype(jnp.bfloat16).astype(jnp.float32)
            key_ref[...] = turn(fresh, cosine, sine).astype(jnp.bfloat16)
        else:
            value_ref[...] = total.astype(jnp.bfloat16)


def tables_kernel(
    length_ref, row_ref, column_ref, inverse_ref, out, place_ref, tables, sems
):
    length, inverse, column = length_ref[0], inverse_ref[...], column_ref[...]
    slots = lax.broadcasted_iota(jnp.int32, (1, HIST), 1)
    place_ref[:, :HIST] = jnp.where(slots < length, -1, FAR)
    place_ref[:, HIST + CONTEXT :] = row_ref[...]

    def sending(step):
        some = pl.ds(pl.multiple_of(step * STEP, STEP), STEP)
        return pltpu.make_async_copy(tables.at[:, some], out.at[:, some], sems.at[step])

    def one(step, _):
        rows = lax.broadcasted_iota(jnp.int32, (STEP, 1), 0)
        base = (step & 1) * (4 * BLOCK) + (step >> 1) * PIECE
        rows = base + (rows >> 7) * BLOCK + (rows & 127)
        at = pl.multiple_of(step * STEP, STEP)
        some = pl.ds(at, STEP)
        tables[0, some], tables[1, some] = waves(rows + length, inverse)
        sending(step).start()
        here = lax.broadcasted_iota(jnp.int32, (1, STEP), 1)
        here = base + (here >> 7) * BLOCK + (here & 127)
        hits = jnp.max(jnp.where(column == here, 1, 0), axis=0, keepdims=True)
        place_ref[:, pl.ds(at + HIST, STEP)] = jnp.where(hits > 0, FAR, here)
        return 0

    lax.fori_loop(0, CONTEXT // STEP, one, 0)
    for step in range(CONTEXT // STEP):
        sending(step).wait()


def weigh_kernel(
    query_ref, raw_ref, tables_ref, place_ref, past_ref, fresh_ref, column_ref,
    out, tables, keys, scores, mass, sems, sem,
):
    def fetching(step):
        some = pl.ds(pl.multiple_of(step * STEP, STEP), STEP)
        return pltpu.make_async_copy(tables_ref.at[:, some], tables.at[:, some], sems.at[step])

    for step in range(CONTEXT // STEP):
        fetching(step).start()
    keys[:HIST] = past_ref[:, :HEAD]
    keys[HIST + CONTEXT :] = fresh_ref[...]

    def rotate(step, _):
        at = pl.multiple_of(step * STEP, STEP)
        some = pl.ds(at, STEP)
        fetching(step).wait()
        key = turn(raw_ref[some].astype(jnp.float32), tables[0, some], tables[1, some])
        keys[pl.ds(at + HIST, STEP)] = key.astype(jnp.bfloat16)
        return 0

    lax.fori_loop(0, CONTEXT // STEP, rotate, 0)
    scores[...] = lax.dot_general(
        query_ref[...], keys[...], (((1,), (1,)), ((), ())), preferred_element_type=jnp.float32
    ) * np.float32(HEAD**-0.5)

    def sending(at):
        return pltpu.make_async_copy(mass.at[pl.ds(at, SEL)], out.at[pl.ds(at, SEL)], sem)

    def soften(step, _):
        at = pl.multiple_of(step * SEL, SEL)
        part = jnp.where(place_ref[...] <= column_ref[...], scores[pl.ds(at, SEL)], -jnp.inf)
        part = jnp.exp(part - jnp.max(part, axis=1, keepdims=True))
        part = part * (1.0 / jnp.sum(part, axis=1, keepdims=True))
        mass[pl.ds(at, SEL)] = part.astype(jnp.bfloat16)
        sending(at).start()
        return 0

    lax.fori_loop(0, QPER, soften, 0)
    for head in range(QPER):
        sending(head * SEL).wait()


def mix_kernel(mass_ref, value_ref, past_ref, fresh_ref, out_ref):
    late = HIST + CONTEXT
    mixed = jnp.dot(mass_ref[:, :HIST], past_ref[:, HEAD:], preferred_element_type=jnp.float32)
    mixed += jnp.dot(mass_ref[:, late:], fresh_ref[...], preferred_element_type=jnp.float32)
    mixed += jnp.dot(mass_ref[:, HIST:late], value_ref[...], preferred_element_type=jnp.float32)
    for head in range(QPER):
        part = mixed[head * SEL : (head + 1) * SEL]
        out_ref[:, head * HEAD : (head + 1) * HEAD] = part.astype(jnp.bfloat16)


def per_device(hidden, w_query, w_key_value, block_kv, history_kv, block_lists, sel_pos, hist_len):
    z = lax.axis_index("z").reshape(1)
    column, inverse = sel_pos[0].reshape(SEL, 1), jnp.asarray(INVERSE).reshape(1, HEAD)
    bf16, f32 = jnp.bfloat16, jnp.float32

    head = lax.axis_index("head").reshape(1)
    both = pl.pallas_call(
        pack_kernel,
        out_shape=jax.ShapeDtypeStruct((256, WIDE), bf16),
        in_specs=[HBM] * 2,
        out_specs=HBM,
        scratch_shapes=[pltpu.VMEM((256, WIDE), bf16), pltpu.SemaphoreType.DMA],
        compiler_params=grant(56),
        cost_estimate=FREE,
    )(w_query, w_key_value)
    shapes = (NX, 2, 2, PIECE, HEAD), (NX, HALF, NZ * 256), (NH, HIST // NH, 256)
    pieces, rows, past = pl.pallas_call(
        prepare_kernel,
        out_shape=[jax.ShapeDtypeStruct(shape, bf16) for shape in shapes],
        in_specs=[SMEM] * 2 + [HBM] * 3,
        out_specs=[HBM] * 3,
        scratch_shapes=[pltpu.VMEM(shape, bf16) for shape in shapes]
        + [pltpu.SemaphoreType.DMA((6,))],
        compiler_params=grant(56),
        cost_estimate=FREE,
    )(z, head, after(hidden[0], both), block_kv, history_kv[0])

    pieces = lax.all_to_all(pieces, "x", 0, 0, tiled=True)
    own = pieces.reshape(NX * 4, PIECE, HEAD)
    w_up, w_down, up, down = [both], [both], [own], [own]
    for step in range(3):
        w_down.append(lax.ppermute(after(w_down[-1], w_up[step]), "z", DOWN))
        w_up.append(lax.ppermute(after(w_up[-1], w_down[max(step - 1, 0)]), "z", UP))
    down.append(lax.ppermute(after(own, w_down[3], w_up[3]), "z", DOWN))
    w_up.append(lax.ppermute(after(w_up[3], w_down[2]), "z", UP))
    received = lax.all_to_all(after(rows, pieces, w_up[1], w_down[1]), "x", 0, 0, tiled=True)
    past = lax.all_to_all(after(past, received), "head", 0, 0, tiled=True).reshape(HIST, 2 * HEAD)
    received = after(received, w_up[3], w_down[3])
    swapped = lax.ppermute(received, "head", [(i, i ^ 1) for i in range(NH)])
    weights = w_down + w_up[:0:-1]
    down.append(lax.ppermute(after(down[1], w_down[3], w_up[3]), "z", DOWN))
    up.append(lax.ppermute(after(own, w_up[4], w_down[3], past), "z", UP))

    partial = pl.pallas_call(
        project_kernel,
        out_shape=jax.ShapeDtypeStruct((NX, SEL, WIDE), f32),
        in_specs=[SMEM] + [ANY] * 2 + [HBM] * NZ,
        out_specs=HBM,
        scratch_shapes=[
            pltpu.VMEM((NZ * 256, WIDE), bf16),
            pltpu.VMEM((NX * SEL, NZ * 256), bf16),
            pltpu.VMEM((NX, SEL, WIDE), f32),
            pltpu.SemaphoreType.DMA((2,)),
        ],
        compiler_params=grant(56),
        cost_estimate=FREE,
    )(head, after(received, past), swapped, *weights)
    up.append(lax.ppermute(after(up[1], down[1], partial), "z", UP))
    up.append(lax.ppermute(after(up[2], down[2]), "z", UP))
    down.append(lax.ppermute(after(down[2], up[1]), "z", DOWN))
    tables, place = pl.pallas_call(
        tables_kernel,
        out_shape=[
            jax.ShapeDtypeStruct((2, CONTEXT, HEAD), f32),
            jax.ShapeDtypeStruct((1, KEYS), jnp.int32),
        ],
        in_specs=[SMEM] + [VMEM] * 3,
        out_specs=[HBM, VMEM],
        scratch_shapes=[
            pltpu.VMEM((2, CONTEXT, HEAD), f32),
            pltpu.SemaphoreType.DMA((CONTEXT // STEP,)),
        ],
        compiler_params=grant(16),
        cost_estimate=FREE,
    )(after(hist_len, down[2]), sel_pos, column, inverse)
    down.append(lax.ppermute(after(down[3], up[2], place), "z", DOWN))
    held = down + up[:0:-1]
    partial = lax.all_to_all(partial, "x", 0, 0, tiled=True)
    queries, fresh_keys, fresh_values = kernel_call(
        queries_kernel,
        [
            jax.ShapeDtypeStruct((QPER * SEL, HEAD), bf16),
            jax.ShapeDtypeStruct((SEL, HEAD), bf16),
            jax.ShapeDtypeStruct((SEL, HEAD), bf16),
        ],
        [hist_len, partial, column, inverse],
        smem=1,
    )

    raw = lax.all_to_all(pick(z, block_lists, held, 0), "x", 0, 0, tiled=True)
    mass = pl.pallas_call(
        weigh_kernel,
        out_shape=jax.ShapeDtypeStruct((QPER * SEL, KEYS), bf16),
        in_specs=[VMEM] * 2 + [HBM] + [VMEM] * 4,
        out_specs=HBM,
        scratch_shapes=[
            pltpu.VMEM((2, CONTEXT, HEAD), f32),
            pltpu.VMEM((KEYS, HEAD), bf16),
            pltpu.VMEM((QPER * SEL, KEYS), f32),
            pltpu.VMEM((QPER * SEL, KEYS), bf16),
            pltpu.SemaphoreType.DMA((CONTEXT // STEP,)),
            pltpu.SemaphoreType.DMA,
        ],
        compiler_params=grant(56),
        cost_estimate=FREE,
    )(queries, raw.reshape(CONTEXT, HEAD), tables, place, past, fresh_keys, column)
    values = lax.all_to_all(pick(after(z, queries), block_lists, held, 1), "x", 0, 0, tiled=True)
    mixed = kernel_call(
        mix_kernel,
        jax.ShapeDtypeStruct((SEL, QPER * HEAD), bf16),
        [mass, values.reshape(CONTEXT, HEAD), past, fresh_values],
    )
    return mixed[None]


def solution(mesh):
    split = Mesh(mesh.devices.reshape(NZ, NX, NH), ("z", "x", "head"))
    store = ("z", "x")
    in_specs = (
        P(store, None, None),
        P(store, "head"),
        P(store, "head"),
        P(store, None, "head"),
        P(store, "head", None),
        P(),
        P(store, None),
        P(store),
    )
    return jax.shard_map(
        per_device, mesh=split, in_specs=in_specs, out_specs=P(store, None, "head"), check_vma=False
    )
```
